32 devices in a mesh: space: 8 (over y, x, core), view: 4 (over z).
Axes of the slice: x: 2, y: 2, z: 4, core: 2. Of those that a mesh axis runs over, the one named last changes fastest.
Arguments:
- estimate: float32 [512, 32, 256], P('space'), may hold values from 0.5 to 2
- images: bfloat16 [8, 512, 32, 256], P('view', 'space'), may hold values from 0.5 to 2
- kernel_halves: float32 [8, 3, 16], P('view'), may hold values from 0.02 to 1
Outputs:
- new_estimate: float32 [512, 32, 256], P('space', 'view')
The draws below stay inside these ranges and needn't reach their ends.
All inputs are finite; a program needn't handle non-finite values.
Results may differ from the reference program's by a relative error of at most 0.0003.
Values sent between devices are 32-bit elements; how exact they have to be, the bound alone decides.
A program may use at most 128 MiB of HBM per device.

```python
import math
import jax
import jax.numpy as jnp
from jax import lax

VIEWS = 8
HALF = 16
XPIX = 32
YPIX = 256
ITERS = 2
NZ = 512


def block_levels(key, dims, shards, smallest, high):
    def one(position, parts):
        heights = jax.random.uniform(jax.random.fold_in(jax.random.fold_in(key, 6), position), (parts,), jnp.float32, smallest / len(shards), high / len(shards))
        return jnp.repeat(jnp.exp(heights), dims[position] // parts).reshape((-1,) + (1,) * (len(dims) - position - 1))

    factor_of = one(*shards[0])
    for cut in shards[1:]:
        factor_of = factor_of * one(*cut)
    return factor_of


def setup_inputs(seed: int = 0) -> dict:
    keys = jax.random.split(jax.random.key(seed), 4)
    estimate = jnp.clip(jnp.exp(math.log(2.0) - 1.3862944 * jax.random.uniform(keys[0], (NZ, XPIX, YPIX), jnp.float32) ** block_levels(keys[0], (NZ, XPIX, YPIX), ((0, 8),), -0.2, 0.2)), 0.5, 2.0)
    images = jnp.clip(jnp.exp(math.log(2.0) - 1.3862944 * jax.random.uniform(keys[1], (VIEWS, NZ, XPIX, YPIX), jnp.float32) ** block_levels(keys[1], (VIEWS, NZ, XPIX, YPIX), ((0, 4), (1, 8)), -0.2, 0.2)), 0.5, 2.0).astype(jnp.bfloat16)
    kernel_halves = jnp.clip(jnp.exp(math.log(1.0) - 3.912023 * jax.random.uniform(keys[2], (VIEWS, 3, HALF), jnp.float32) ** block_levels(keys[2], (VIEWS, 3, HALF), ((0, 4),), -0.2, 0.2)), 0.02, 1.0)
    return {"estimate": estimate, "images": images, "kernel_halves": kernel_halves}


def normalize(kernel_halves):
    kernel_sum = kernel_halves[..., 0] + 2.0 * jnp.sum(kernel_halves[..., 1:], axis=-1)
    return kernel_halves / kernel_sum[..., None]


def smooth_axis(field, kernel_row, axis_number):
    radius = kernel_row.shape[0] - 1
    length = field.shape[axis_number]
    widths = [(0, 0), (0, 0), (0, 0)]
    widths[axis_number] = (radius, radius)
    padded = jnp.pad(field, widths)
    result = jnp.zeros(field.shape, jnp.float32)
    for offset in range(2 * radius + 1):
        weight = kernel_row[abs(offset - radius)]
        result = result + weight * lax.slice_in_dim(padded, offset, offset + length, axis=axis_number)
    return result


def blur(field, kernel_set):
    result = smooth_axis(field, kernel_set[2], 2)
    result = smooth_axis(result, kernel_set[1], 1)
    return smooth_axis(result, kernel_set[0], 0)


def reference(estimate, images, kernel_halves):
    kernels = normalize(kernel_halves)
    current = estimate
    for iteration in range(ITERS):
        def accumulate(product, inputs):
            picture, kernel_set = inputs
            blurred = blur(current, kernel_set)
            quotient = picture.astype(jnp.float32) / blurred
            return product * blur(quotient, kernel_set), None

        combined, unused = lax.scan(accumulate, jnp.ones(current.shape, jnp.float32), (images, kernels))
        current = current * combined
    return current
```

```python
import functools

import jax
import jax.numpy as jnp
from jax import lax
from jax.experimental import pallas as pl
from jax.experimental.pallas import tpu as pltpu
from jax.sharding import PartitionSpec as P

ITERS = 2
MARGIN = 16
UNIT = 16
STEP = 8
MESH = pl.DeviceIdType.MESH
F32, BF16 = jnp.float32, jnp.bfloat16
ORDERS = ((1, 2, 0, 3), (2, 1, 0, 3))


def halved(t):
    hi = t.astype(BF16)
    return hi, (t - hi.astype(F32)).astype(BF16)


def thirds(t):
    hi = t.astype(BF16)
    rest = t - hi.astype(F32)
    mid = rest.astype(BF16)
    return hi, mid, (rest - mid.astype(F32)).astype(BF16)


def dot(a, b):
    return jnp.dot(a, b, preferred_element_type=F32)


def aligned(start, multiple=STEP):
    return start if isinstance(start, int) else pl.multiple_of(start, multiple)


def kernel(dims, est_hbm, img_hbm, halves, out, cur, mid, smooth, fac, from_l, from_r, to_r, to_l, eland, est, img,
           ty, cx, dm, pm, local_sem, est_send, est_recv, halo_send, halo_recv, edge_send, edge_recv,
           send_r, recv_l, send_l, recv_r):
    n, planes, wx, wy, views, taps = dims
    me = lax.axis_index("view")
    spot, spots = lax.axis_index("space"), lax.axis_size("space")
    has_down, has_up = spot > 0, spot < spots - 1
    has_left, has_right = me > 0, me < n - 1
    up = {"space": jnp.minimum(spot + 1, spots - 1)}
    down = {"space": jnp.maximum(spot - 1, 0)}
    right = {"view": jnp.minimum(me + 1, n - 1)}
    left = {"view": jnp.maximum(me - 1, 0)}
    rows = wx // n
    tile = wx * STEP
    far = MARGIN + planes

    est_copy = pltpu.make_async_copy(est_hbm, est, local_sem.at[0])
    img_copy = pltpu.make_async_copy(img_hbm, img, local_sem.at[1])
    est_copy.start()
    img_copy.start()

    barrier = pltpu.get_barrier_semaphore()
    count = 0
    for there, who in ((has_down, down), (has_up, up), (has_left, left), (has_right, right)):
        @pl.when(there)
        def _(who=who):
            pl.semaphore_signal(barrier, inc=1, device_id=who, device_id_type=MESH)
        count = count + there.astype(jnp.int32)
    pl.semaphore_wait(barrier, count)

    def est_to(side):
        first = 0 if side == 1 else (planes - MARGIN) * wx
        return pltpu.make_async_remote_copy(
            est_hbm.at[pl.ds(first, MARGIN * wx)], eland.at[side], est_send.at[side], est_recv.at[side],
            device_id=up if side == 0 else down, device_id_type=MESH)

    def smooth_to(it, side):
        src, dst = ((far - MARGIN, 0), (MARGIN, far))[side]
        return pltpu.make_async_remote_copy(
            smooth.at[it, :, :, pl.ds(src, MARGIN)], smooth.at[it, :, :, pl.ds(dst, MARGIN)],
            halo_send.at[it, side], halo_recv.at[it, side],
            device_id=up if side == 0 else down, device_id_type=MESH)

    def edge_to(side, h, k):
        src, dst = ((far - MARGIN, 0), (MARGIN, far))[side]
        xs = pl.ds(k * rows, rows)
        return pltpu.make_async_remote_copy(
            cur.at[1, xs, pl.ds(aligned(src + h * STEP), STEP)], cur.at[1, xs, pl.ds(aligned(dst + h * STEP), STEP)],
            edge_send.at[side, h * n + k], edge_recv.at[side, h * n + k],
            device_id=up if side == 0 else down, device_id_type=MESH)

    sends = ((has_up, has_down), (has_down, has_up))

    for side in range(2):
        @pl.when(sends[side][0])
        def _(side=side):
            est_to(side).start()

    def taps_at(distance, v, a, spacing=1):
        side = halves[v, a, 1]
        for j in range(2, taps):
            side = side + halves[v, a, j]
        total = jnp.full(distance.shape, halves[v, a, 0] + 2.0 * side)
        matrix = jnp.zeros(distance.shape, F32)
        for j in range(taps):
            matrix = jnp.where(distance == j * spacing, halves[v, a, j], matrix)
        return matrix / total

    block = 32

    def build(b, carry):
        start = pl.multiple_of(b * block, block)
        spots_in = pl.ds(start, block)
        r = lax.broadcasted_iota(jnp.int32, (block, wy), 0) + start
        c = lax.broadcasted_iota(jnp.int32, (block, wy), 1)
        for v in range(views):
            hi, lo = halved(taps_at(jnp.abs(r - c), v, 2))
            for part, value in enumerate((hi, hi, lo)):
                ty[v, pl.ds(pl.multiple_of(part * wy + start, block), block), :] = value
        r = lax.broadcasted_iota(jnp.int32, (block, tile), 0) + start
        c = lax.broadcasted_iota(jnp.int32, (block, tile), 1)
        for v in range(views):
            hi, lo = halved(taps_at(jnp.abs(r - c), v, 1, STEP))
            for part, value in enumerate((hi, hi, lo)):
                cx[v, spots_in, pl.ds(part * tile, tile)] = value
        one = jnp.where(c == (r % STEP) * wx + r // STEP, 1.0, 0.0).astype(BF16)
        for part in range(3):
            pm[spots_in, pl.ds(part * tile, tile)] = one
        return carry

    assert wy == tile
    lax.fori_loop(0, wy // block, build, 0)

    window = UNIT + 2 * MARGIN
    p = lax.broadcasted_iota(jnp.int32, (UNIT, 4 * window), 0)
    c = lax.broadcasted_iota(jnp.int32, (UNIT, 4 * window), 1)
    for v in range(views):
        value = taps_at(jnp.abs(c % window - MARGIN - p), v, 0)
        for x in range(2):
            hi, lo = halved(jnp.where((c // window) % 2 == x, value, 0.0))
            dm[pl.ds(v * 4 * UNIT + x * UNIT, UNIT), :] = hi
            dm[pl.ds(v * 4 * UNIT + (2 + x) * UNIT, UNIT), :] = lo

    for side, start in ((0, 0), (1, far)):
        @pl.when(jnp.logical_not(sends[side][1]))
        def _(start=start):
            def clear(x, carry):
                zero = jnp.zeros((MARGIN, wy), F32)
                for it in range(ITERS):
                    cur[it, x, pl.ds(start, MARGIN), :] = zero
                    for v in range(views):
                        smooth[it, v, x, pl.ds(start, MARGIN), :] = zero
                return carry
            lax.fori_loop(0, wx, clear, 0)

    def turned(values):
        return dot(pm[...], jnp.concatenate(thirds(values), 0)).reshape(wx, STEP, wy)

    est_copy.wait()

    def turn_own(b, carry):
        values = est[pl.ds(pl.multiple_of(b * tile, tile), tile), :]
        cur[0, :, pl.ds(pl.multiple_of(MARGIN + b * STEP, STEP), STEP), :] = turned(values)
        return carry

    lax.fori_loop(0, planes // STEP, turn_own, 0, unroll=2)
    img_copy.wait()

    def turn_halo(side):
        @pl.when(sends[side][1])
        def _():
            est_to(side).wait_recv()
            for b in range(MARGIN // STEP):
                start = (0, far)[side] + b * STEP
                cur[0, :, pl.ds(start, STEP), :] = turned(eland[side, pl.ds(b * tile, tile), :])

    def deep_first(it, u):
        def body(j, carry):
            x = 2 * j
            values = cur[it, pl.ds(x, 2), pl.ds(aligned(UNIT * u), window), :].reshape(2 * window, wy)
            got = dot(dm[...], jnp.concatenate(halved(values), 0)).reshape(views, 2, 2, UNIT, wy)
            for v in range(views):
                mid[v, pl.ds(x, 2)] = got[v, 0] + got[v, 1]
            return carry
        lax.fori_loop(0, wx // 2, body, 0, unroll=4)

    def along_y(t, v):
        hi, lo = halved(t)
        return dot(jnp.concatenate([hi, lo, hi], 1), ty[v])

    def along_x(t, v):
        hi, lo = halved(t)
        return dot(cx[v], jnp.concatenate([hi, lo, hi], 0))

    def planar(it, u):
        todo = [(v, h) for h in range(UNIT // STEP) for v in range(views)]
        ts = [mid[v, :, pl.ds(h * STEP, STEP), :].reshape(tile, wy) for v, h in todo]
        ts = [along_y(t, v) for t, (v, h) in zip(ts, todo)]
        ts = [along_x(t, v) for t, (v, h) in zip(ts, todo)]
        pics = [dot(pm[:, :tile], img[v, pl.ds(aligned((u * UNIT + h * STEP) * wx, tile), tile), :]) for v, h in todo]
        ts = [pic / t for t, pic in zip(ts, pics)]
        ts = [along_x(t, v) for t, (v, h) in zip(ts, todo)]
        ts = [along_y(t, v) for t, (v, h) in zip(ts, todo)]
        for t, (v, h) in zip(ts, todo):
            smooth[it, v, :, pl.ds(aligned(MARGIN + u * UNIT + h * STEP), STEP), :] = t.reshape(wx, STEP, wy)

    def forward(it, u):
        deep_first(it, u)
        planar(it, u)

    def deep_last(it, u):
        def body(j, carry):
            x = 2 * j
            got = []
            for v in range(views):
                values = smooth[it, v, pl.ds(x, 2), pl.ds(aligned(UNIT * u), window), :].reshape(2 * window, wy)
                part = dot(dm[pl.ds(v * 4 * UNIT, 4 * UNIT), :], jnp.concatenate(halved(values), 0))
                got.append(part[:2 * UNIT] + part[2 * UNIT:])
            product = got[0]
            for more in got[1:]:
                product = product * more
            fac[pl.ds(x, 2), pl.ds(aligned(UNIT * u), UNIT), :] = product.reshape(2, UNIT, wy)
            return carry
        lax.fori_loop(0, wx // 2, body, 0, unroll=4)

    per_unit = n * (UNIT // STEP)
    items = n * (planes // STEP)

    def place(it, i, goes_left):
        order = ORDERS[it]
        q, h, k = i // per_unit, (i // n) % (UNIT // STEP), i % n
        if it == ITERS - 1 and not goes_left:
            k = n - 1 - k
        u = order[-1]
        for pos in range(len(order) - 1):
            u = jnp.where(q == pos, order[pos], u)
        return u, h, k, pl.ds(k * rows, rows), u * UNIT + h * STEP

    def hop(it, goes_left, xs, ps, i):
        buf_out, buf_in, s, r, who = (
            (to_l, from_r, send_l, recv_r, left) if goes_left else (to_r, from_l, send_r, recv_l, right))
        return pltpu.make_async_remote_copy(
            buf_out.at[xs, ps], buf_in.at[it, xs, ps], s.at[it, i], r.at[it, i], device_id=who, device_id_type=MESH)

    def pass_on(it, i, goes_left):
        _, _, k, xs, first = place(it, i, goes_left)
        ps = pl.ds(aligned(first), STEP)
        live = (i >= 0) & (i < items)
        buf_out, buf_in = (to_l, from_r) if goes_left else (to_r, from_l)
        has_from, has_to = (has_right, has_left) if goes_left else (has_left, has_right)
        if it == ITERS - 1:
            wants = k <= me if goes_left else k >= me
            beyond = k < me if goes_left else k > me
        else:
            wants = beyond = True

        @pl.when(live & has_from & wants)
        def _():
            hop(it, goes_left, xs, ps, i).wait_recv()

        @pl.when(live & has_to & beyond)
        def _():
            @pl.when(has_from)
            def _():
                buf_out[xs, ps, :] = buf_in[it, xs, ps, :] * fac[xs, ps, :]

            @pl.when(jnp.logical_not(has_from))
            def _():
                buf_out[xs, ps, :] = fac[xs, ps, :]

            hop(it, goes_left, xs, ps, i).start()

    def conclude(it, i):
        u, h, k, xs, first = place(it, i, True)
        ps = pl.ds(aligned(first), STEP)
        inner = pl.ds(aligned(MARGIN + first), STEP)
        live = (i >= 0) & (i < items)
        if it == ITERS - 1:
            live = live & (k == me)

        def finish(with_left, with_right):
            total = fac[xs, ps, :] * cur[it, xs, inner, :]
            if with_left:
                total = total * from_l[it, xs, ps, :]
            if with_right:
                total = total * from_r[it, xs, ps, :]
            if it == ITERS - 1:
                out[:, ps, :] = total
            else:
                cur[it + 1, xs, inner, :] = total

        @pl.when(live & jnp.logical_not(has_left))
        def _():
            finish(False, True)

        @pl.when(live & has_left & has_right)
        def _():
            finish(True, True)

        @pl.when(live & jnp.logical_not(has_right))
        def _():
            finish(True, False)

        if it < ITERS - 1:
            @pl.when(live & (u == planes // UNIT - 1) & has_up)
            def _():
                edge_to(0, h, k).start()

            @pl.when(live & (u == 0) & has_down)
            def _():
                edge_to(1, h, k).start()

    def steps(it, begin, end):
        def step(s, carry):
            pass_on(it, s - me, False)
            pass_on(it, s - (n - 1 - me), True)
            if it == ITERS - 1:
                group = s // n
                conclude_now = s % n == n - 1

                @pl.when(conclude_now)
                def _():
                    conclude(it, group * n + me)
            else:
                conclude(it, s - (n - 1))
            return carry
        lax.fori_loop(begin, end, step, 0)

    def settle(it):
        def body(i, carry):
            for goes_left in (False, True):
                _, _, k, xs, first = place(it, i, goes_left)
                ps = pl.ds(aligned(first), STEP)
                has_to = has_left if goes_left else has_right
                beyond = True
                if it == ITERS - 1:
                    beyond = k < me if goes_left else k > me

                @pl.when(has_to & beyond)
                def _():
                    hop(it, goes_left, xs, ps, i).wait_send()
            return carry
        lax.fori_loop(0, items, body, 0)

    def send_smooth(it, side):
        @pl.when(sends[side][0])
        def _():
            smooth_to(it, side).start()

    def get_smooth(it, side):
        @pl.when(sends[side][1])
        def _():
            smooth_to(it, side).wait_recv()

    def get_edge(side):
        @pl.when(sends[side][1])
        def _():
            for h in range(MARGIN // STEP):
                for k in range(n):
                    edge_to(side, h, k).wait_recv()

    forward(0, 1)
    forward(0, 2)
    turn_halo(0)
    forward(0, 0)
    send_smooth(0, 1)
    deep_last(0, 1)
    steps(0, 0, 1)
    turn_halo(1)
    forward(0, 3)
    send_smooth(0, 0)
    steps(0, 1, 2)
    deep_last(0, 2)
    steps(0, 2, 16)
    get_smooth(0, 0)
    deep_last(0, 0)
    steps(0, 16, 24)
    get_smooth(0, 1)
    deep_last(0, 3)
    steps(0, 24, items + n - 1)
    settle(0)

    forward(1, 1)
    forward(1, 2)
    get_edge(1)
    forward(1, 3)
    send_smooth(1, 0)
    deep_last(1, 2)
    steps(1, 0, 1)
    get_edge(0)
    forward(1, 0)
    send_smooth(1, 1)
    steps(1, 1, 2)
    deep_last(1, 1)
    steps(1, 2, 16)
    get_smooth(1, 0)
    deep_last(1, 0)
    steps(1, 16, 24)
    get_smooth(1, 1)
    deep_last(1, 3)
    steps(1, 24, items)
    settle(1)

    for side in range(2):
        @pl.when(sends[side][0])
        def _(side=side):
            est_to(side).wait_send()
            for it in range(ITERS):
                smooth_to(it, side).wait_send()
            for h in range(MARGIN // STEP):
                for k in range(n):
                    edge_to(side, h, k).wait_send()


def solution(mesh):
    n = mesh.shape["view"]

    def on_device(estimate, images, kernel_halves):
        planes, wx, wy = estimate.shape
        views, _, taps = kernel_halves.shape
        rows, tile = wx // n, wx * STEP
        items = n * (planes // STEP)
        deep = planes + 2 * MARGIN
        window = UNIT + 2 * MARGIN
        vmem = pltpu.VMEM
        dma = pltpu.SemaphoreType.DMA
        slab = vmem((wx, planes, wy), F32)
        landing = vmem((ITERS, wx, planes, wy), F32)
        result = pl.pallas_call(
            functools.partial(kernel, (n, planes, wx, wy, views, taps)),
            out_shape=jax.ShapeDtypeStruct((rows, planes, wy), F32),
            in_specs=[pl.BlockSpec(memory_space=pl.ANY), pl.BlockSpec(memory_space=pl.ANY),
                      pl.BlockSpec(memory_space=pltpu.SMEM)],
            out_specs=pl.BlockSpec(memory_space=pltpu.VMEM),
            scratch_shapes=[
                vmem((ITERS, wx, deep, wy), F32),
                vmem((views, wx, UNIT, wy), F32),
                vmem((ITERS, views, wx, deep, wy), F32),
                slab, landing, landing, slab, slab,
                vmem((2, MARGIN * wx, wy), F32),
                vmem((planes * wx, wy), F32),
                vmem((views, planes * wx, wy), BF16),
                vmem((views, 3 * wy, wy), BF16),
                vmem((views, tile, 3 * tile), BF16),
                vmem((views * 4 * UNIT, 4 * window), BF16),
                vmem((tile, 3 * tile), BF16),
                dma((2,)), dma((2,)), dma((2,)),
                dma((ITERS, 2)), dma((ITERS, 2)),
                dma((2, items // 4)), dma((2, items // 4)),
                dma((ITERS, items)), dma((ITERS, items)), dma((ITERS, items)), dma((ITERS, items)),
            ],
            compiler_params=pltpu.CompilerParams(
                collective_id=1, has_side_effects=True, vmem_limit_bytes=56 << 20),
            cost_estimate=pl.CostEstimate(flops=20 << 30, bytes_accessed=5 << 20, transcendentals=0),
        )(estimate.reshape(planes * wx, wy), images.reshape(views, planes * wx, wy), kernel_halves)
        return result.transpose(1, 0, 2)

    placed = (P("space", None, None), P("view", "space", None, None), P("view", None, None))
    return jax.shard_map(
        on_device, mesh=mesh, in_specs=placed, out_specs=P("space", "view", None), check_vma=False
    )
```

```python
import functools

import jax
import jax.numpy as jnp
from jax import lax
from jax.experimental import pallas as pl
from jax.experimental.pallas import tpu as pltpu
from jax.sharding import PartitionSpec as P

ITERS = 2
MARGIN = 16
UNIT = 16
STEP = 8
LAG = 4
MESH = pl.DeviceIdType.MESH
F32, BF16 = jnp.float32, jnp.bfloat16
ORDERS = ((1, 2, 0, 3), (2, 1, 0, 3))


def halved(t):
    hi = t.astype(BF16)
    return hi, (t - hi.astype(F32)).astype(BF16)


def thirds(t):
    hi = t.astype(BF16)
    rest = t - hi.astype(F32)
    mid = rest.astype(BF16)
    return hi, mid, (rest - mid.astype(F32)).astype(BF16)


def dot(a, b):
    return jnp.dot(a, b, preferred_element_type=F32)


def aligned(start, multiple=STEP):
    return start if isinstance(start, int) else pl.multiple_of(start, multiple)


def kernel(dims, est_hbm, img_hbm, halves, out, cur, mid, smooth, fac, from_l, from_r, to_r, to_l, eland, est, img,
           ty, cx, dm, pm, local_sem, est_send, est_recv, halo_send, halo_recv, edge_send, edge_recv,
           send_r, recv_l, send_l, recv_r):
    n, planes, wx, wy, views, taps = dims
    me = lax.axis_index("view")
    spot, spots = lax.axis_index("space"), lax.axis_size("space")
    has_down, has_up = spot > 0, spot < spots - 1
    has_left, has_right = me > 0, me < n - 1
    up = {"space": jnp.minimum(spot + 1, spots - 1)}
    down = {"space": jnp.maximum(spot - 1, 0)}
    right = {"view": jnp.minimum(me + 1, n - 1)}
    left = {"view": jnp.maximum(me - 1, 0)}
    rows = wx // n
    tile = wx * STEP
    far = MARGIN + planes

    est_copy = pltpu.make_async_copy(est_hbm, est, local_sem.at[0])
    img_copy = pltpu.make_async_copy(img_hbm, img, local_sem.at[1])
    est_copy.start()
    img_copy.start()

    barrier = pltpu.get_barrier_semaphore()
    count = 0
    for there, who in ((has_down, down), (has_up, up), (has_left, left), (has_right, right)):
        @pl.when(there)
        def _(who=who):
            pl.semaphore_signal(barrier, inc=1, device_id=who, device_id_type=MESH)
        count = count + there.astype(jnp.int32)
    pl.semaphore_wait(barrier, count)

    def est_to(side):
        first = 0 if side == 1 else (planes - MARGIN) * wx
        return pltpu.make_async_remote_copy(
            est_hbm.at[pl.ds(first, MARGIN * wx)], eland.at[side], est_send.at[side], est_recv.at[side],
            device_id=up if side == 0 else down, device_id_type=MESH)

    def smooth_to(it, side):
        src, dst = ((far - MARGIN, 0), (MARGIN, far))[side]
        return pltpu.make_async_remote_copy(
            smooth.at[it, :, :, pl.ds(src, MARGIN)], smooth.at[it, :, :, pl.ds(dst, MARGIN)],
            halo_send.at[it, side], halo_recv.at[it, side],
            device_id=up if side == 0 else down, device_id_type=MESH)

    def edge_to(side, h, k):
        src, dst = ((far - MARGIN, 0), (MARGIN, far))[side]
        xs = pl.ds(k * rows, rows)
        return pltpu.make_async_remote_copy(
            cur.at[1, xs, pl.ds(aligned(src + h * STEP), STEP)], cur.at[1, xs, pl.ds(aligned(dst + h * STEP), STEP)],
            edge_send.at[side, h * n + k], edge_recv.at[side, h * n + k],
            device_id=up if side == 0 else down, device_id_type=MESH)

    sends = ((has_up, has_down), (has_down, has_up))

    for side in range(2):
        @pl.when(sends[side][0])
        def _(side=side):
            est_to(side).start()

    def taps_at(distance, v, a, spacing=1):
        side = halves[v, a, 1]
        for j in range(2, taps):
            side = side + halves[v, a, j]
        total = jnp.full(distance.shape, halves[v, a, 0] + 2.0 * side)
        matrix = jnp.zeros(distance.shape, F32)
        for j in range(taps):
            matrix = jnp.where(distance == j * spacing, halves[v, a, j], matrix)
        return matrix / total

    block = 32

    def build(b, carry):
        start = pl.multiple_of(b * block, block)
        spots_in = pl.ds(start, block)
        r = lax.broadcasted_iota(jnp.int32, (block, wy), 0) + start
        c = lax.broadcasted_iota(jnp.int32, (block, wy), 1)
        for v in range(views):
            hi, lo = halved(taps_at(jnp.abs(r - c), v, 2))
            for part, value in enumerate((hi, hi, lo)):
                ty[v, pl.ds(pl.multiple_of(part * wy + start, block), block), :] = value
        r = lax.broadcasted_iota(jnp.int32, (block, tile), 0) + start
        c = lax.broadcasted_iota(jnp.int32, (block, tile), 1)
        for v in range(views):
            hi, lo = halved(taps_at(jnp.abs(r - c), v, 1, STEP))
            for part, value in enumerate((hi, hi, lo)):
                cx[v, spots_in, pl.ds(part * tile, tile)] = value
        one = jnp.where(c == (r % STEP) * wx + r // STEP, 1.0, 0.0).astype(BF16)
        for part in range(3):
            pm[spots_in, pl.ds(part * tile, tile)] = one
        return carry

    assert wy == tile
    lax.fori_loop(0, wy // block, build, 0)

    window = UNIT + 2 * MARGIN
    p = lax.broadcasted_iota(jnp.int32, (UNIT, 4 * window), 0)
    c = lax.broadcasted_iota(jnp.int32, (UNIT, 4 * window), 1)
    for v in range(views):
        value = taps_at(jnp.abs(c % window - MARGIN - p), v, 0)
        for x in range(2):
            hi, lo = halved(jnp.where((c // window) % 2 == x, value, 0.0))
            dm[pl.ds(v * 4 * UNIT + x * UNIT, UNIT), :] = hi
            dm[pl.ds(v * 4 * UNIT + (2 + x) * UNIT, UNIT), :] = lo

    for side, start in ((0, 0), (1, far)):
        @pl.when(jnp.logical_not(sends[side][1]))
        def _(start=start):
            def clear(x, carry):
                zero = jnp.zeros((MARGIN, wy), F32)
                for it in range(ITERS):
                    cur[it, x, pl.ds(start, MARGIN), :] = zero
                    for v in range(views):
                        smooth[it, v, x, pl.ds(start, MARGIN), :] = zero
                return carry
            lax.fori_loop(0, wx, clear, 0)

    def turned(values):
        return dot(pm[...], jnp.concatenate(thirds(values), 0)).reshape(wx, STEP, wy)

    est_copy.wait()

    def turn_own(b, carry):
        values = est[pl.ds(pl.multiple_of(b * tile, tile), tile), :]
        cur[0, :, pl.ds(pl.multiple_of(MARGIN + b * STEP, STEP), STEP), :] = turned(values)
        return carry

    lax.fori_loop(0, planes // STEP, turn_own, 0, unroll=2)
    img_copy.wait()

    def turn_halo(side):
        @pl.when(sends[side][1])
        def _():
            est_to(side).wait_recv()
            for b in range(MARGIN // STEP):
                start = (0, far)[side] + b * STEP
                cur[0, :, pl.ds(start, STEP), :] = turned(eland[side, pl.ds(b * tile, tile), :])

    def deep_first(it, u):
        def body(j, carry):
            x = 2 * j
            values = cur[it, pl.ds(x, 2), pl.ds(aligned(UNIT * u), window), :].reshape(2 * window, wy)
            got = dot(dm[...], jnp.concatenate(halved(values), 0)).reshape(views, 2, 2, UNIT, wy)
            for v in range(views):
                mid[v, pl.ds(x, 2)] = got[v, 0] + got[v, 1]
            return carry
        lax.fori_loop(0, wx // 2, body, 0, unroll=4)

    def along_y(t, v):
        hi, lo = halved(t)
        return dot(jnp.concatenate([hi, lo, hi], 1), ty[v])

    def along_x(t, v):
        hi, lo = halved(t)
        return dot(cx[v], jnp.concatenate([hi, lo, hi], 0))

    def planar(it, u):
        todo = [(v, h) for h in range(UNIT // STEP) for v in range(views)]
        ts = [mid[v, :, pl.ds(h * STEP, STEP), :].reshape(tile, wy) for v, h in todo]
        ts = [along_y(t, v) for t, (v, h) in zip(ts, todo)]
        ts = [along_x(t, v) for t, (v, h) in zip(ts, todo)]
        pics = [dot(pm[:, :tile], img[v, pl.ds(aligned((u * UNIT + h * STEP) * wx, tile), tile), :]) for v, h in todo]
        ts = [pic / t for t, pic in zip(ts, pics)]
        ts = [along_x(t, v) for t, (v, h) in zip(ts, todo)]
        ts = [along_y(t, v) for t, (v, h) in zip(ts, todo)]
        for t, (v, h) in zip(ts, todo):
            smooth[it, v, :, pl.ds(aligned(MARGIN + u * UNIT + h * STEP), STEP), :] = t.reshape(wx, STEP, wy)

    def forward(it, u):
        deep_first(it, u)
        planar(it, u)

    def deep_last(it, u):
        def body(j, carry):
            x = 2 * j
            got = []
            for v in range(views):
                values = smooth[it, v, pl.ds(x, 2), pl.ds(aligned(UNIT * u), window), :].reshape(2 * window, wy)
                part = dot(dm[pl.ds(v * 4 * UNIT, 4 * UNIT), :], jnp.concatenate(halved(values), 0))
                got.append(part[:2 * UNIT] + part[2 * UNIT:])
            product = got[0]
            for more in got[1:]:
                product = product * more
            fac[pl.ds(x, 2), pl.ds(aligned(UNIT * u), UNIT), :] = product.reshape(2, UNIT, wy)
            return carry
        lax.fori_loop(0, wx // 2, body, 0, unroll=4)

    per_unit = n * (UNIT // STEP)
    items = n * (planes // STEP)

    def place(it, i, goes_left):
        order = ORDERS[it]
        q, h, k = i // per_unit, (i // n) % (UNIT // STEP), i % n
        if it == ITERS - 1 and not goes_left:
            k = n - 1 - k
        u = order[-1]
        for pos in range(len(order) - 1):
            u = jnp.where(q == pos, order[pos], u)
        return u, h, k, pl.ds(k * rows, rows), u * UNIT + h * STEP

    def hop(it, goes_left, i):
        buf_out, buf_in, s, r, who = (
            (to_l, from_r, send_l, recv_r, left) if goes_left else (to_r, from_l, send_r, recv_l, right))
        return pltpu.make_async_remote_copy(
            buf_out.at[i], buf_in.at[it, i], s.at[it, i], r.at[it, i], device_id=who, device_id_type=MESH)

    def pass_on(it, i, goes_left):
        _, _, k, xs, first = place(it, i, goes_left)
        ps = pl.ds(aligned(first), STEP)
        live = (i >= 0) & (i < items)
        buf_out, buf_in = (to_l, from_r) if goes_left else (to_r, from_l)
        has_from, has_to = (has_right, has_left) if goes_left else (has_left, has_right)
        if it == ITERS - 1:
            wants = k <= me if goes_left else k >= me
            beyond = k < me if goes_left else k > me
        else:
            wants = beyond = True

        @pl.when(live & has_from & wants)
        def _():
            hop(it, goes_left, i).wait_recv()

        @pl.when(live & has_to & beyond)
        def _():
            @pl.when(has_from)
            def _():
                buf_out[i] = buf_in[it, i] * fac[xs, ps, :]

            @pl.when(jnp.logical_not(has_from))
            def _():
                buf_out[i] = fac[xs, ps, :]

            hop(it, goes_left, i).start()

    def conclude(it, i):
        u, h, k, xs, first = place(it, i, True)
        ps = pl.ds(aligned(first), STEP)
        inner = pl.ds(aligned(MARGIN + first), STEP)
        live = (i >= 0) & (i < items)
        from_left_at = i
        if it == ITERS - 1:
            from_left_at = i + n - 1 - 2 * k

        def finish(with_left, with_right):
            total = fac[xs, ps, :] * cur[it, xs, inner, :]
            if with_left:
                total = total * from_l[it, from_left_at]
            if with_right:
                total = total * from_r[it, i]
            if it == ITERS - 1:
                out[:, ps, :] = total
            else:
                cur[it + 1, xs, inner, :] = total

        @pl.when(live & jnp.logical_not(has_left))
        def _():
            finish(False, True)

        @pl.when(live & has_left & has_right)
        def _():
            finish(True, True)

        @pl.when(live & jnp.logical_not(has_right))
        def _():
            finish(True, False)

        if it < ITERS - 1:
            @pl.when(live & (u == planes // UNIT - 1) & has_up)
            def _():
                edge_to(0, h, k).start()

            @pl.when(live & (u == 0) & has_down)
            def _():
                edge_to(1, h, k).start()

    def steps(it, begin, end):
        def step(s, carry):
            pass_on(it, s - LAG * me, False)
            pass_on(it, s - LAG * (n - 1 - me), True)
            done = s - LAG * (n - 1)
            if it == ITERS - 1:
                @pl.when((done >= 0) & (done % n == 0))
                def _():
                    conclude(it, done + me)
            else:
                conclude(it, done)
            return carry
        lax.fori_loop(begin, end, step, 0)

    def settle(it):
        def body(i, carry):
            for goes_left in (False, True):
                _, _, k, _, _ = place(it, i, goes_left)
                has_to = has_left if goes_left else has_right
                beyond = True
                if it == ITERS - 1:
                    beyond = k < me if goes_left else k > me

                @pl.when(has_to & beyond)
                def _():
                    hop(it, goes_left, i).wait_send()
            return carry
        lax.fori_loop(0, items, body, 0)

    def send_smooth(it, side):
        @pl.when(sends[side][0])
        def _():
            smooth_to(it, side).start()

    def get_smooth(it, side):
        @pl.when(sends[side][1])
        def _():
            smooth_to(it, side).wait_recv()

    def get_edge(side):
        @pl.when(sends[side][1])
        def _():
            for h in range(MARGIN // STEP):
                for k in range(n):
                    edge_to(side, h, k).wait_recv()

    forward(0, 1)
    forward(0, 2)
    turn_halo(0)
    forward(0, 0)
    send_smooth(0, 1)
    deep_last(0, 1)
    steps(0, 0, 1)
    turn_halo(1)
    forward(0, 3)
    send_smooth(0, 0)
    steps(0, 1, 2)
    deep_last(0, 2)
    steps(0, 2, 16)
    get_smooth(0, 0)
    deep_last(0, 0)
    steps(0, 16, 24)
    get_smooth(0, 1)
    deep_last(0, 3)
    steps(0, 24, items + LAG * (n - 1))
    settle(0)

    forward(1, 1)
    forward(1, 2)
    get_edge(1)
    forward(1, 3)
    send_smooth(1, 0)
    deep_last(1, 2)
    steps(1, 0, 1)
    get_edge(0)
    forward(1, 0)
    send_smooth(1, 1)
    steps(1, 1, 2)
    deep_last(1, 1)
    steps(1, 2, 16)
    get_smooth(1, 0)
    deep_last(1, 0)
    steps(1, 16, 24)
    get_smooth(1, 1)
    deep_last(1, 3)
    steps(1, 24, items + LAG * (n - 1))
    settle(1)

    for side in range(2):
        @pl.when(sends[side][0])
        def _(side=side):
            est_to(side).wait_send()
            for it in range(ITERS):
                smooth_to(it, side).wait_send()
            for h in range(MARGIN // STEP):
                for k in range(n):
                    edge_to(side, h, k).wait_send()


def solution(mesh):
    n = mesh.shape["view"]

    def on_device(estimate, images, kernel_halves):
        planes, wx, wy = estimate.shape
        views, _, taps = kernel_halves.shape
        rows, tile = wx // n, wx * STEP
        items = n * (planes // STEP)
        deep = planes + 2 * MARGIN
        window = UNIT + 2 * MARGIN
        vmem = pltpu.VMEM
        dma = pltpu.SemaphoreType.DMA
        slab = vmem((wx, planes, wy), F32)
        outgoing = vmem((items, rows, STEP, wy), F32)
        landing = vmem((ITERS, items, rows, STEP, wy), F32)
        result = pl.pallas_call(
            functools.partial(kernel, (n, planes, wx, wy, views, taps)),
            out_shape=jax.ShapeDtypeStruct((rows, planes, wy), F32),
            in_specs=[pl.BlockSpec(memory_space=pl.ANY), pl.BlockSpec(memory_space=pl.ANY),
                      pl.BlockSpec(memory_space=pltpu.SMEM)],
            out_specs=pl.BlockSpec(memory_space=pltpu.VMEM),
            scratch_shapes=[
                vmem((ITERS, wx, deep, wy), F32),
                vmem((views, wx, UNIT, wy), F32),
                vmem((ITERS, views, wx, deep, wy), F32),
                slab, landing, landing, outgoing, outgoing,
                vmem((2, MARGIN * wx, wy), F32),
                vmem((planes * wx, wy), F32),
                vmem((views, planes * wx, wy), BF16),
                vmem((views, 3 * wy, wy), BF16),
                vmem((views, tile, 3 * tile), BF16),
                vmem((views * 4 * UNIT, 4 * window), BF16),
                vmem((tile, 3 * tile), BF16),
                dma((2,)), dma((2,)), dma((2,)),
                dma((ITERS, 2)), dma((ITERS, 2)),
                dma((2, n * (MARGIN // STEP))), dma((2, n * (MARGIN // STEP))),
                dma((ITERS, items)), dma((ITERS, items)), dma((ITERS, items)), dma((ITERS, items)),
            ],
            compiler_params=pltpu.CompilerParams(
                collective_id=1, has_side_effects=True, vmem_limit_bytes=56 << 20),
            cost_estimate=pl.CostEstimate(flops=20 << 30, bytes_accessed=5 << 20, transcendentals=0),
        )(estimate.reshape(planes * wx, wy), images.reshape(views, planes * wx, wy), kernel_halves)
        return result.transpose(1, 0, 2)

    placed = (P("space", None, None), P("view", "space", None, None), P("view", None, None))
    return jax.shard_map(
        on_device, mesh=mesh, in_specs=placed, out_specs=P("space", "view", None), check_vma=False
    )
```

```python
import functools

import jax
import jax.numpy as jnp
from jax import lax
from jax.experimental import pallas as pl
from jax.experimental.pallas import tpu as pltpu
from jax.sharding import PartitionSpec as P

ITERS = 2
MARGIN = 16
UNIT = 16
STEP = 8
LAG = 5
MESH = pl.DeviceIdType.MESH
F32, BF16 = jnp.float32, jnp.bfloat16
NEAR, FAR = 0, 1


def halved(t):
    hi = t.astype(BF16)
    return hi, (t - hi.astype(F32)).astype(BF16)


def thirds(t):
    hi = t.astype(BF16)
    rest = t - hi.astype(F32)
    mid = rest.astype(BF16)
    return hi, mid, (rest - mid.astype(F32)).astype(BF16)


def dot(a, b):
    return jnp.dot(a, b, preferred_element_type=F32)


def aligned(start, multiple=STEP):
    return start if isinstance(start, int) else pl.multiple_of(start, multiple)


def kernel(dims, est_hbm, img_hbm, halves, out, cur, mid, smooth, fac, from_l, from_r, to_r, to_l, eland, est, img,
           ty, cx, dm, dm8, pm, back, local_sem, est_send, est_recv, halo_send, halo_recv, edge_send, edge_recv,
           send_r, recv_l, send_l, recv_r):
    n, planes, wx, wy, views, taps = dims
    me = lax.axis_index("view")
    spot, spots = lax.axis_index("space"), lax.axis_size("space")
    odd = spot % 2 == 1
    toward = jnp.where(odd, -1, 1)
    there = (spot + toward < spots, (spot - toward >= 0) & (spot - toward < spots))
    who = ({"space": jnp.minimum(spot + toward, spots - 1)}, {"space": jnp.clip(spot - toward, 0, spots - 1)})
    has_left, has_right = me > 0, me < n - 1
    right = {"view": jnp.minimum(me + 1, n - 1)}
    left = {"view": jnp.maximum(me - 1, 0)}
    rows = wx // n
    tile = wx * STEP
    deep = planes + 2 * MARGIN

    def unit(f):
        return jnp.where(odd, f, planes // UNIT - 1 - f)

    margin_at = (jnp.where(odd, 0, deep - MARGIN), jnp.where(odd, deep - MARGIN, 0))
    border_at = (jnp.where(odd, MARGIN, deep - 2 * MARGIN), jnp.where(odd, deep - 2 * MARGIN, MARGIN))
    lands_at = (margin_at[FAR], margin_at[NEAR])

    est_copy = pltpu.make_async_copy(est_hbm, est, local_sem.at[0])
    img_copy = pltpu.make_async_copy(img_hbm, img, local_sem.at[1])
    est_copy.start()
    img_copy.start()

    barrier = pltpu.get_barrier_semaphore()
    count = 0
    for here, device in ((there[NEAR], who[NEAR]), (there[FAR], who[FAR]), (has_left, left), (has_right, right)):
        @pl.when(here)
        def _(device=device):
            pl.semaphore_signal(barrier, inc=1, device_id=device, device_id_type=MESH)
        count = count + here.astype(jnp.int32)

    def est_to(side):
        first = (border_at[side] - MARGIN) * wx
        return pltpu.make_async_remote_copy(
            est_hbm.at[pl.ds(aligned(first, MARGIN * wx), MARGIN * wx)], eland.at[side],
            est_send.at[side], est_recv.at[side], device_id=who[side], device_id_type=MESH)

    def piece_at(side, piece):
        return jnp.where(odd == ((side == FAR) == (piece == 0)), STEP, 0)

    def smooth_to(it, side, piece):
        off = piece_at(side, piece)
        return pltpu.make_async_remote_copy(
            smooth.at[it, :, :, pl.ds(aligned(border_at[side] + off), STEP)],
            smooth.at[it, :, :, pl.ds(aligned(lands_at[side] + off), STEP)],
            halo_send.at[it, side, piece], halo_recv.at[it, side, piece], device_id=who[side], device_id_type=MESH)

    def smooth_from(it, side, piece):
        into = smooth.at[it, :, :, pl.ds(aligned(margin_at[side] + STEP - piece_at(side, piece)), STEP)]
        return pltpu.make_async_remote_copy(
            into, into, halo_send.at[it, side, piece], halo_recv.at[it, side, piece],
            device_id=who[side], device_id_type=MESH)

    def edge_to(side, h, k, to=lands_at):
        xs = pl.ds(k * rows, rows)
        return pltpu.make_async_remote_copy(
            cur.at[1, xs, pl.ds(aligned(border_at[side] + h * STEP), STEP)],
            cur.at[1, xs, pl.ds(aligned(to[side] + h * STEP), STEP)],
            edge_send.at[side, h * n + k], edge_recv.at[side, h * n + k],
            device_id=who[side], device_id_type=MESH)

    def taps_at(distance, v, a, spacing=1):
        side = halves[a, v, 1]
        for j in range(2, taps):
            side = side + halves[a, v, j]
        total = jnp.full(distance.shape, halves[a, v, 0] + 2.0 * side)
        matrix = jnp.zeros(distance.shape, F32)
        for j in range(taps):
            matrix = jnp.where(distance == j * spacing, halves[a, v, j], matrix)
        return matrix / total

    block = 32

    def build(b, carry):
        start = pl.multiple_of(b * block, block)
        spots_in = pl.ds(start, block)
        r = lax.broadcasted_iota(jnp.int32, (block, wy), 0) + start
        c = lax.broadcasted_iota(jnp.int32, (block, wy), 1)
        for v in range(views):
            hi, lo = halved(taps_at(jnp.abs(r - c), v, 2))
            for part, value in enumerate((hi, hi, lo)):
                ty[v, pl.ds(pl.multiple_of(part * wy + start, block), block), :] = value
        r = lax.broadcasted_iota(jnp.int32, (block, tile), 0) + start
        c = lax.broadcasted_iota(jnp.int32, (block, tile), 1)
        for v in range(views):
            hi, lo = halved(taps_at(jnp.abs(r - c), v, 1, STEP))
            for part, value in enumerate((hi, hi, lo)):
                cx[v, spots_in, pl.ds(part * tile, tile)] = value
        one = jnp.where(c == (r % STEP) * wx + r // STEP, 1.0, 0.0).astype(BF16)
        for part in range(3):
            pm[spots_in, pl.ds(part * tile, tile)] = one
        return carry

    assert wy == tile
    lax.fori_loop(0, wy // block, build, 0)

    for size, into in ((UNIT, dm), (STEP, dm8)):
        width = size + 2 * MARGIN
        p = lax.broadcasted_iota(jnp.int32, (size, 4 * width), 0)
        c = lax.broadcasted_iota(jnp.int32, (size, 4 * width), 1)
        for v in range(views):
            value = taps_at(jnp.abs(c % width - MARGIN - p), v, 0)
            parts = [halved(jnp.where((c // width) % 2 == x, value, 0.0)) for x in range(2)]
            into[pl.ds(v * 4 * size, 4 * size), :] = jnp.concatenate(
                [parts[0][0], parts[1][0], parts[0][1], parts[1][1]], 0)
    window = UNIT + 2 * MARGIN
    square = rows * STEP
    r = lax.broadcasted_iota(jnp.int32, (square, 3 * square), 0)
    c = lax.broadcasted_iota(jnp.int32, (square, 3 * square), 1) % square
    back[...] = jnp.where(c == (r % rows) * STEP + r // rows, 1.0, 0.0).astype(BF16)

    pl.semaphore_wait(barrier, count)
    for side in (FAR, NEAR):
        @pl.when(there[side])
        def _(side=side):
            est_to(side).start()

    for side in (NEAR, FAR):
        @pl.when(jnp.logical_not(there[side]))
        def _(start=aligned(margin_at[side], MARGIN)):
            def clear(x, carry):
                zero = jnp.zeros((MARGIN, wy), F32)
                for it in range(ITERS):
                    cur[it, x, pl.ds(start, MARGIN), :] = zero
                    for v in range(views):
                        smooth[it, v, x, pl.ds(start, MARGIN), :] = zero
                return carry
            lax.fori_loop(0, wx, clear, 0)

    def turned(values):
        return dot(pm[...], jnp.concatenate(thirds(values), 0)).reshape(wx, STEP, wy)

    est_copy.wait()

    def turn_own(g, carry):
        b = jnp.where(odd, g, planes // STEP - 1 - g)
        values = est[pl.ds(pl.multiple_of(b * tile, tile), tile), :]
        cur[0, :, pl.ds(pl.multiple_of(MARGIN + b * STEP, STEP), STEP), :] = turned(values)
        return carry

    def turn_halo(side):
        @pl.when(there[side])
        def _():
            est_to(side).wait_recv()
            for b in range(MARGIN // STEP):
                start = aligned(margin_at[side] + b * STEP)
                cur[0, :, pl.ds(start, STEP), :] = turned(eland[side, pl.ds(b * tile, tile), :])

    def deep_first(it, u):
        def body(j, carry):
            x = 2 * j
            values = cur[it, pl.ds(x, 2), pl.ds(aligned(UNIT * u), window), :].reshape(2 * window, wy)
            got = dot(dm[...], jnp.concatenate(halved(values), 0)).reshape(views, 2, 2, UNIT, wy)
            for v in range(views):
                mid[v, pl.ds(x, 2)] = got[v, 0] + got[v, 1]
            return carry
        lax.fori_loop(0, wx // 2, body, 0, unroll=4)

    def along_y(t, v):
        hi, lo = halved(t)
        return dot(jnp.concatenate([hi, lo, hi], 1), ty[v])

    def along_x(t, v):
        hi, lo = halved(t)
        return dot(cx[v], jnp.concatenate([hi, lo, hi], 0))

    def planar(it, u):
        todo = [(v, h) for h in range(UNIT // STEP) for v in range(views)]
        ts = [mid[v, :, pl.ds(h * STEP, STEP), :].reshape(tile, wy) for v, h in todo]
        ts = [along_y(t, v) for t, (v, h) in zip(ts, todo)]
        ts = [along_x(t, v) for t, (v, h) in zip(ts, todo)]
        pics = [dot(pm[:, :tile], img[v, pl.ds(aligned((u * UNIT + h * STEP) * wx, tile), tile), :]) for v, h in todo]
        ts = [pic / t for t, pic in zip(ts, pics)]
        ts = [along_x(t, v) for t, (v, h) in zip(ts, todo)]
        ts = [along_y(t, v) for t, (v, h) in zip(ts, todo)]
        for t, (v, h) in zip(ts, todo):
            smooth[it, v, :, pl.ds(aligned(MARGIN + u * UNIT + h * STEP), STEP), :] = t.reshape(wx, STEP, wy)

    def forward(it, u):
        deep_first(it, u)
        planar(it, u)

    def deep_last(it, f, part=None):
        size, matrix = (UNIT, dm) if part is None else (STEP, dm8)
        start = unit(f) * UNIT
        if part is not None:
            start = start + jnp.where(odd == (part == 1), STEP, 0)
        width = size + 2 * MARGIN

        def body(j, carry):
            x = 2 * j
            got = []
            for v in range(views):
                values = smooth[it, v, pl.ds(x, 2), pl.ds(aligned(start), width), :].reshape(2 * width, wy)
                both = dot(matrix[pl.ds(v * 4 * size, 4 * size), :], jnp.concatenate(halved(values), 0))
                got.append(both[:2 * size] + both[2 * size:])
            product = got[0]
            for more in got[1:]:
                product = product * more
            fac[pl.ds(x, 2), pl.ds(aligned(start), size), :] = product.reshape(2, size, wy)
            return carry
        lax.fori_loop(0, wx // 2, body, 0, unroll=4)

    per_unit = n * (UNIT // STEP)
    items = n * (planes // STEP)

    def place(it, i, goes_left):
        f, h, k = i // per_unit, (i // n) % (UNIT // STEP), i % n
        if it == ITERS - 1 and not goes_left:
            k = n - 1 - k
        h = jnp.where(odd, h, UNIT // STEP - 1 - h)
        return f, h, k, pl.ds(k * rows, rows), unit(f) * UNIT + h * STEP

    def hop(it, goes_left, i):
        buf_out, buf_in, s, r, who = (
            (to_l, from_r, send_l, recv_r, left) if goes_left else (to_r, from_l, send_r, recv_l, right))
        return pltpu.make_async_remote_copy(
            buf_out.at[it, i], buf_in.at[it, i], s.at[it], r.at[it, i], device_id=who, device_id_type=MESH)

    def pass_on(it, i, goes_left):
        _, _, k, xs, first = place(it, i, goes_left)
        ps = pl.ds(aligned(first), STEP)
        live = (i >= 0) & (i < items)
        buf_out, buf_in = (to_l, from_r) if goes_left else (to_r, from_l)
        has_from, has_to = (has_right, has_left) if goes_left else (has_left, has_right)
        if it == ITERS - 1:
            wants = k <= me if goes_left else k >= me
            beyond = k < me if goes_left else k > me
        else:
            wants = beyond = True

        @pl.when(live & has_from & wants)
        def _():
            hop(it, goes_left, i).wait_recv()

        @pl.when(live & has_to & beyond)
        def _():
            @pl.when(has_from)
            def _():
                buf_out[it, i] = buf_in[it, i] * fac[xs, ps, :]

            @pl.when(jnp.logical_not(has_from))
            def _():
                buf_out[it, i] = fac[xs, ps, :]

            hop(it, goes_left, i).start()

    def conclude(it, i):
        f, h, k, xs, first = place(it, i, True)
        ps = pl.ds(aligned(first), STEP)
        inner = pl.ds(aligned(MARGIN + first), STEP)
        live = (i >= 0) & (i < items)
        from_left_at = i
        if it == ITERS - 1:
            from_left_at = i + n - 1 - 2 * k

        def finish(with_left, with_right):
            total = fac[xs, ps, :] * cur[it, xs, inner, :]
            if with_left:
                total = total * from_l[it, from_left_at]
            if with_right:
                total = total * from_r[it, i]
            if it == ITERS - 1:
                turned_back = dot(back[...], jnp.concatenate(thirds(total.reshape(rows * STEP, wy)), 0))
                out[pl.ds(aligned(first * rows), rows * STEP), :] = turned_back
            else:
                cur[it + 1, xs, inner, :] = total

        @pl.when(live & jnp.logical_not(has_left))
        def _():
            finish(False, True)

        @pl.when(live & has_left & has_right)
        def _():
            finish(True, True)

        @pl.when(live & jnp.logical_not(has_right))
        def _():
            finish(True, False)

        if it < ITERS - 1:
            for side, border in ((NEAR, 0), (FAR, planes // UNIT - 1)):
                @pl.when(live & (f == border) & there[side])
                def _(side=side):
                    edge_to(side, h, k).start()

    def advance(it, s):
        pass_on(it, s - LAG * me, False)
        pass_on(it, s - LAG * (n - 1 - me), True)
        done = s - LAG * (n - 1)
        if it == ITERS - 1:
            @pl.when((done >= 0) & (done % n == 0))
            def _():
                conclude(it, done + me)
        else:
            conclude(it, done)

    def steps(begin, end, *runs):
        def step(s, carry):
            for it, first in runs:
                advance(it, s + first)
            return carry
        lax.fori_loop(begin, end, step, 0)

    def settle(it):
        for goes_left, buf, sem in ((False, to_r, send_r), (True, to_l, send_l)):
            for place_in in range(n):
                hops = place_in if goes_left else n - 1 - place_in
                if hops == 0:
                    continue
                sent = items if it < ITERS - 1 else hops * (items // n)

                @pl.when(me == place_in)
                def _(goes_left=goes_left, buf=buf, sem=sem, sent=sent):
                    whole = buf.at[it, pl.ds(0, sent)]
                    pltpu.make_async_copy(whole, whole, sem.at[it]).wait()

    def send_smooth(it, side):
        @pl.when(there[side])
        def _():
            for piece in range(2):
                smooth_to(it, side, piece).start()

    def get_smooth(it, side, piece):
        @pl.when(there[side])
        def _():
            smooth_from(it, side, piece).wait_recv()

    def get_edge(side):
        @pl.when(there[side])
        def _():
            for h in range(MARGIN // STEP):
                for k in range(n):
                    edge_to(side, h, k, margin_at).wait_recv()

    drain = LAG * (n - 1)
    last = planes // STEP - 2
    lax.fori_loop(0, last, turn_own, 0, unroll=2)
    img_copy.wait()
    forward(0, unit(1))
    turn_halo(NEAR)
    forward(0, unit(0))
    send_smooth(0, NEAR)
    lax.fori_loop(last, planes // STEP, turn_own, 0, unroll=2)
    deep_first(0, unit(2))
    get_smooth(0, NEAR, 0)
    get_smooth(0, NEAR, 1)
    deep_last(0, 0)
    steps(0, LAG, (0, 0))
    planar(0, unit(2))
    deep_last(0, 1)
    steps(LAG, LAG + 2, (0, 0))
    turn_halo(FAR)
    forward(0, unit(3))
    send_smooth(0, FAR)
    steps(LAG + 2, LAG + 5, (0, 0))
    deep_last(0, 2)
    half = per_unit // 2
    steps(LAG + 5, 3 * per_unit, (0, 0))
    get_smooth(0, FAR, 0)
    deep_last(0, 3, 0)
    steps(3 * per_unit, 3 * per_unit + half, (0, 0))
    get_smooth(0, FAR, 1)
    deep_last(0, 3, 1)
    steps(3 * per_unit + half, 2 * per_unit + drain, (0, 0))

    get_edge(NEAR)
    forward(1, unit(0))
    send_smooth(1, NEAR)
    steps(2 * per_unit + drain, 3 * per_unit + drain, (0, 0))
    forward(1, unit(1))
    get_smooth(1, NEAR, 0)
    get_smooth(1, NEAR, 1)
    deep_last(1, 0)
    steps(0, per_unit, (0, 3 * per_unit + drain), (1, 0))
    forward(1, unit(2))
    deep_last(1, 1)
    steps(per_unit, per_unit + 2, (1, 0))
    get_edge(FAR)
    forward(1, unit(3))
    send_smooth(1, FAR)
    steps(per_unit + 2, per_unit + 4, (1, 0))
    deep_last(1, 2)
    steps(per_unit + 4, 3 * per_unit, (1, 0))
    get_smooth(1, FAR, 0)
    deep_last(1, 3, 0)
    steps(3 * per_unit, 3 * per_unit + half, (1, 0))
    get_smooth(1, FAR, 1)
    deep_last(1, 3, 1)
    steps(3 * per_unit + half, items + drain, (1, 0))
    settle(0)
    settle(1)

    for side in (NEAR, FAR):
        @pl.when(there[side])
        def _(side=side):
            est_to(side).wait_send()
            for it in range(ITERS):
                for piece in range(2):
                    smooth_to(it, side, piece).wait_send()
            for h in range(MARGIN // STEP):
                for k in range(n):
                    edge_to(side, h, k).wait_send()


def solution(mesh):
    n = mesh.shape["view"]

    def on_device(estimate, images, kernel_halves):
        planes, wx, wy = estimate.shape
        views, _, taps = kernel_halves.shape
        rows, tile = wx // n, wx * STEP
        items = n * (planes // STEP)
        deep = planes + 2 * MARGIN
        vmem = pltpu.VMEM
        dma = pltpu.SemaphoreType.DMA
        slab = vmem((wx, planes, wy), F32)
        landing = vmem((ITERS, items, rows, STEP, wy), F32)
        result = pl.pallas_call(
            functools.partial(kernel, (n, planes, wx, wy, views, taps)),
            out_shape=jax.ShapeDtypeStruct((planes * rows, wy), F32),
            in_specs=[pl.BlockSpec(memory_space=pl.ANY), pl.BlockSpec(memory_space=pl.ANY),
                      pl.BlockSpec(memory_space=pltpu.SMEM)],
            out_specs=pl.BlockSpec(memory_space=pltpu.VMEM),
            scratch_shapes=[
                vmem((ITERS, wx, deep, wy), F32),
                vmem((views, wx, UNIT, wy), F32),
                vmem((ITERS, views, wx, deep, wy), F32),
                slab, landing, landing, landing, landing,
                vmem((2, MARGIN * wx, wy), F32),
                vmem((planes * wx, wy), F32),
                vmem((views, planes * wx, wy), BF16),
                vmem((views, 3 * wy, wy), BF16),
                vmem((views, tile, 3 * tile), BF16),
                vmem((views * 4 * UNIT, 4 * (UNIT + 2 * MARGIN)), BF16),
                vmem((views * 4 * STEP, 4 * (STEP + 2 * MARGIN)), BF16),
                vmem((tile, 3 * tile), BF16),
                vmem((rows * STEP, 3 * rows * STEP), BF16),
                dma((2,)), dma((2,)), dma((2,)),
                dma((ITERS, 2, 2)), dma((ITERS, 2, 2)),
                dma((2, n * (MARGIN // STEP))), dma((2, n * (MARGIN // STEP))),
                dma((ITERS,)), dma((ITERS, items)), dma((ITERS,)), dma((ITERS, items)),
            ],
            compiler_params=pltpu.CompilerParams(
                collective_id=1, has_side_effects=True, vmem_limit_bytes=56 << 20),
            cost_estimate=pl.CostEstimate(flops=20 << 30, bytes_accessed=5 << 20, transcendentals=0),
        )(estimate.reshape(planes * wx, wy), images.reshape(views, planes * wx, wy), kernel_halves.transpose(1, 0, 2))
        return result.reshape(planes, rows, wy)

    placed = (P("space", None, None), P("view", "space", None, None), P("view", None, None))
    return jax.shard_map(
        on_device, mesh=mesh, in_specs=placed, out_specs=P("space", "view", None), check_vma=False
    )
```

```python
import functools

import jax
import jax.numpy as jnp
from jax import lax
from jax.experimental import pallas as pl
from jax.experimental.pallas import tpu as pltpu
from jax.sharding import PartitionSpec as P

ITERS = 2
MARGIN = 16
UNIT = 16
STEP = 8
LAG, SLACK = 3, 0
MESH = pl.DeviceIdType.MESH
F32, BF16 = jnp.float32, jnp.bfloat16
NEAR, FAR = 0, 1


def halved(t):
    hi = t.astype(BF16)
    return hi, (t - hi.astype(F32)).astype(BF16)


def thirds(t):
    hi = t.astype(BF16)
    rest = t - hi.astype(F32)
    mid = rest.astype(BF16)
    return hi, mid, (rest - mid.astype(F32)).astype(BF16)


def dot(a, b):
    return jnp.dot(a, b, preferred_element_type=F32)


def aligned(start, multiple=STEP):
    return start if isinstance(start, int) else pl.multiple_of(start, multiple)


def kernel(dims, est_hbm, img_hbm, halves, out, cur, mid, smooth, fac, from_l, from_r, to_r, to_l, eland, est, img,
           ty, cx, dm, dm8, pm, back, local_sem, est_send, est_recv, halo_send, halo_recv, edge_send, edge_recv,
           send_r, recv_l, send_l, recv_r):
    n, planes, wx, wy, views, taps = dims
    me = lax.axis_index("view")
    spot, spots = lax.axis_index("space"), lax.axis_size("space")
    odd = spot % 2 == 1
    toward = jnp.where(odd, -1, 1)
    there = (spot + toward < spots, (spot - toward >= 0) & (spot - toward < spots))
    who = ({"space": jnp.minimum(spot + toward, spots - 1)}, {"space": jnp.clip(spot - toward, 0, spots - 1)})
    has_left, has_right = me > 0, me < n - 1
    right = {"view": jnp.minimum(me + 1, n - 1)}
    left = {"view": jnp.maximum(me - 1, 0)}
    rows = wx // n
    tile = wx * STEP
    deep = planes + 2 * MARGIN

    def unit(f):
        return jnp.where(odd, f, planes // UNIT - 1 - f)

    margin_at = (jnp.where(odd, 0, deep - MARGIN), jnp.where(odd, deep - MARGIN, 0))
    border_at = (jnp.where(odd, MARGIN, deep - 2 * MARGIN), jnp.where(odd, deep - 2 * MARGIN, MARGIN))
    lands_at = (margin_at[FAR], margin_at[NEAR])

    est_copy = pltpu.make_async_copy(est_hbm, est, local_sem.at[0])
    img_copy = pltpu.make_async_copy(img_hbm, img, local_sem.at[1])
    est_copy.start()
    img_copy.start()

    barrier = pltpu.get_barrier_semaphore()
    count = 0
    for here, device in ((there[NEAR], who[NEAR]), (there[FAR], who[FAR]), (has_left, left), (has_right, right)):
        @pl.when(here)
        def _(device=device):
            pl.semaphore_signal(barrier, inc=1, device_id=device, device_id_type=MESH)
        count = count + here.astype(jnp.int32)

    def est_to(side):
        first = (border_at[side] - MARGIN) * wx
        return pltpu.make_async_remote_copy(
            est_hbm.at[pl.ds(aligned(first, MARGIN * wx), MARGIN * wx)], eland.at[side],
            est_send.at[side], est_recv.at[side], device_id=who[side], device_id_type=MESH)

    def piece_at(side, piece):
        return jnp.where(odd == ((side == FAR) == (piece == 0)), STEP, 0)

    def smooth_to(it, side, piece):
        off = piece_at(side, piece)
        return pltpu.make_async_remote_copy(
            smooth.at[it, :, :, pl.ds(aligned(border_at[side] + off), STEP)],
            smooth.at[it, :, :, pl.ds(aligned(lands_at[side] + off), STEP)],
            halo_send.at[it, side, piece], halo_recv.at[it, side, piece], device_id=who[side], device_id_type=MESH)

    def smooth_from(it, side, piece):
        into = smooth.at[it, :, :, pl.ds(aligned(margin_at[side] + STEP - piece_at(side, piece)), STEP)]
        return pltpu.make_async_remote_copy(
            into, into, halo_send.at[it, side, piece], halo_recv.at[it, side, piece],
            device_id=who[side], device_id_type=MESH)

    def edge_to(side, h, k, to=lands_at):
        xs = pl.ds(k * rows, rows)
        return pltpu.make_async_remote_copy(
            cur.at[1, xs, pl.ds(aligned(border_at[side] + h * STEP), STEP)],
            cur.at[1, xs, pl.ds(aligned(to[side] + h * STEP), STEP)],
            edge_send.at[side, h * n + k], edge_recv.at[side, h * n + k],
            device_id=who[side], device_id_type=MESH)

    def taps_at(distance, v, a, spacing=1):
        side = halves[a, v, 1]
        for j in range(2, taps):
            side = side + halves[a, v, j]
        total = jnp.full(distance.shape, halves[a, v, 0] + 2.0 * side)
        matrix = jnp.zeros(distance.shape, F32)
        for j in range(taps):
            matrix = jnp.where(distance == j * spacing, halves[a, v, j], matrix)
        return matrix / total

    block = 32

    def build(b, carry):
        start = pl.multiple_of(b * block, block)
        spots_in = pl.ds(start, block)
        r = lax.broadcasted_iota(jnp.int32, (block, wy), 0) + start
        c = lax.broadcasted_iota(jnp.int32, (block, wy), 1)
        for v in range(views):
            hi, lo = halved(taps_at(jnp.abs(r - c), v, 2))
            for part, value in enumerate((hi, hi, lo)):
                ty[v, pl.ds(pl.multiple_of(part * wy + start, block), block), :] = value
        r = lax.broadcasted_iota(jnp.int32, (block, tile), 0) + start
        c = lax.broadcasted_iota(jnp.int32, (block, tile), 1)
        for v in range(views):
            hi, lo = halved(taps_at(jnp.abs(r - c), v, 1, STEP))
            for part, value in enumerate((hi, hi, lo)):
                cx[v, spots_in, pl.ds(part * tile, tile)] = value
        one = jnp.where(c == (r % STEP) * wx + r // STEP, 1.0, 0.0).astype(BF16)
        for part in range(3):
            pm[spots_in, pl.ds(part * tile, tile)] = one
        return carry

    assert wy == tile
    lax.fori_loop(0, wy // block, build, 0)

    for size, into in ((UNIT, dm), (STEP, dm8)):
        width = size + 2 * MARGIN
        p = lax.broadcasted_iota(jnp.int32, (size, 4 * width), 0)
        c = lax.broadcasted_iota(jnp.int32, (size, 4 * width), 1)
        for v in range(views):
            value = taps_at(jnp.abs(c % width - MARGIN - p), v, 0)
            parts = [halved(jnp.where((c // width) % 2 == x, value, 0.0)) for x in range(2)]
            into[pl.ds(v * 4 * size, 4 * size), :] = jnp.concatenate(
                [parts[0][0], parts[1][0], parts[0][1], parts[1][1]], 0)
    window = UNIT + 2 * MARGIN
    square = rows * STEP
    r = lax.broadcasted_iota(jnp.int32, (square, 3 * square), 0)
    c = lax.broadcasted_iota(jnp.int32, (square, 3 * square), 1) % square
    back[...] = jnp.where(c == (r % rows) * STEP + r // rows, 1.0, 0.0).astype(BF16)

    pl.semaphore_wait(barrier, count)
    for side in (FAR, NEAR):
        @pl.when(there[side])
        def _(side=side):
            est_to(side).start()

    for side in (NEAR, FAR):
        @pl.when(jnp.logical_not(there[side]))
        def _(start=aligned(margin_at[side], MARGIN)):
            def clear(x, carry):
                zero = jnp.zeros((MARGIN, wy), F32)
                for it in range(ITERS):
                    cur[it, x, pl.ds(start, MARGIN), :] = zero
                    for v in range(views):
                        smooth[it, v, x, pl.ds(start, MARGIN), :] = zero
                return carry
            lax.fori_loop(0, wx, clear, 0)

    def turned(values):
        return dot(pm[...], jnp.concatenate(thirds(values), 0)).reshape(wx, STEP, wy)

    est_copy.wait()

    def turn_own(g, carry):
        b = jnp.where(odd, g, planes // STEP - 1 - g)
        values = est[pl.ds(pl.multiple_of(b * tile, tile), tile), :]
        cur[0, :, pl.ds(pl.multiple_of(MARGIN + b * STEP, STEP), STEP), :] = turned(values)
        return carry

    def turn_halo(side):
        @pl.when(there[side])
        def _():
            est_to(side).wait_recv()
            for b in range(MARGIN // STEP):
                start = aligned(margin_at[side] + b * STEP)
                cur[0, :, pl.ds(start, STEP), :] = turned(eland[side, pl.ds(b * tile, tile), :])

    def deep_first(it, u):
        def body(j, carry):
            x = 2 * j
            values = cur[it, pl.ds(x, 2), pl.ds(aligned(UNIT * u), window), :].reshape(2 * window, wy)
            got = dot(dm[...], jnp.concatenate(halved(values), 0)).reshape(views, 2, 2, UNIT, wy)
            for v in range(views):
                mid[v, pl.ds(x, 2)] = got[v, 0] + got[v, 1]
            return carry
        lax.fori_loop(0, wx // 2, body, 0, unroll=16)

    def along_y(t, v):
        hi, lo = halved(t)
        return dot(jnp.concatenate([hi, lo, hi], 1), ty[v])

    def along_x(t, v):
        hi, lo = halved(t)
        return dot(cx[v], jnp.concatenate([hi, lo, hi], 0))

    def planar(it, u):
        todo = [(v, h) for h in range(UNIT // STEP) for v in range(views)]
        ts = [mid[v, :, pl.ds(h * STEP, STEP), :].reshape(tile, wy) for v, h in todo]
        ts = [along_y(t, v) for t, (v, h) in zip(ts, todo)]
        ts = [along_x(t, v) for t, (v, h) in zip(ts, todo)]
        pics = [dot(pm[:, :tile], img[v, pl.ds(aligned((u * UNIT + h * STEP) * wx, tile), tile), :]) for v, h in todo]
        ts = [pic / t for t, pic in zip(ts, pics)]
        ts = [along_x(t, v) for t, (v, h) in zip(ts, todo)]
        ts = [along_y(t, v) for t, (v, h) in zip(ts, todo)]
        for t, (v, h) in zip(ts, todo):
            smooth[it, v, :, pl.ds(aligned(MARGIN + u * UNIT + h * STEP), STEP), :] = t.reshape(wx, STEP, wy)

    def forward(it, u):
        deep_first(it, u)
        planar(it, u)

    def deep_last(it, f, part=None):
        size, matrix = (UNIT, dm) if part is None else (STEP, dm8)
        start = unit(f) * UNIT
        if part is not None:
            start = start + jnp.where(odd == (part == 1), STEP, 0)
        width = size + 2 * MARGIN

        def body(j, carry):
            x = 2 * j
            got = []
            for v in range(views):
                values = smooth[it, v, pl.ds(x, 2), pl.ds(aligned(start), width), :].reshape(2 * width, wy)
                both = dot(matrix[pl.ds(v * 4 * size, 4 * size), :], jnp.concatenate(halved(values), 0))
                got.append(both[:2 * size] + both[2 * size:])
            product = got[0]
            for more in got[1:]:
                product = product * more
            fac[pl.ds(x, 2), pl.ds(aligned(start), size), :] = product.reshape(2, size, wy)
            return carry
        lax.fori_loop(0, wx // 2, body, 0, unroll=16)

    per_unit = n * (UNIT // STEP)
    items = n * (planes // STEP)

    def place(it, i, goes_left):
        f, h, k = i // per_unit, (i // n) % (UNIT // STEP), i % n
        if it == ITERS - 1 and not goes_left:
            k = n - 1 - k
        h = jnp.where(odd, h, UNIT // STEP - 1 - h)
        return f, h, k, pl.ds(k * rows, rows), unit(f) * UNIT + h * STEP

    def hop(it, goes_left, i):
        buf_out, buf_in, s, r, who = (
            (to_l, from_r, send_l, recv_r, left) if goes_left else (to_r, from_l, send_r, recv_l, right))
        return pltpu.make_async_remote_copy(
            buf_out.at[it, i], buf_in.at[it, i], s.at[it], r.at[it, i], device_id=who, device_id_type=MESH)

    def pass_on(it, i, goes_left):
        _, _, k, xs, first = place(it, i, goes_left)
        ps = pl.ds(aligned(first), STEP)
        live = (i >= 0) & (i < items)
        buf_out, buf_in = (to_l, from_r) if goes_left else (to_r, from_l)
        has_from, has_to = (has_right, has_left) if goes_left else (has_left, has_right)
        if it == ITERS - 1:
            wants = k <= me if goes_left else k >= me
            beyond = k < me if goes_left else k > me
        else:
            wants = beyond = True

        @pl.when(live & has_from & wants)
        def _():
            hop(it, goes_left, i).wait_recv()

        @pl.when(live & has_to & beyond)
        def _():
            @pl.when(has_from)
            def _():
                buf_out[it, i] = buf_in[it, i] * fac[xs, ps, :]

            @pl.when(jnp.logical_not(has_from))
            def _():
                buf_out[it, i] = fac[xs, ps, :]

            hop(it, goes_left, i).start()

    def conclude(it, i):
        f, h, k, xs, first = place(it, i, True)
        ps = pl.ds(aligned(first), STEP)
        inner = pl.ds(aligned(MARGIN + first), STEP)
        live = (i >= 0) & (i < items)
        from_left_at = i
        if it == ITERS - 1:
            from_left_at = i + n - 1 - 2 * k

        def finish(with_left, with_right):
            total = fac[xs, ps, :] * cur[it, xs, inner, :]
            if with_left:
                total = total * from_l[it, from_left_at]
            if with_right:
                total = total * from_r[it, i]
            if it == ITERS - 1:
                turned_back = dot(back[...], jnp.concatenate(thirds(total.reshape(rows * STEP, wy)), 0))
                out[pl.ds(aligned(first * rows), rows * STEP), :] = turned_back
            else:
                cur[it + 1, xs, inner, :] = total

        @pl.when(live & jnp.logical_not(has_left))
        def _():
            finish(False, True)

        @pl.when(live & has_left & has_right)
        def _():
            finish(True, True)

        @pl.when(live & jnp.logical_not(has_right))
        def _():
            finish(True, False)

        if it < ITERS - 1:
            for side, border in ((NEAR, 0), (FAR, planes // UNIT - 1)):
                @pl.when(live & (f == border) & there[side])
                def _(side=side):
                    edge_to(side, h, k).start()

    drain = SLACK + LAG * (n - 1)
    ahead = SLACK + LAG

    def advance(it, s):
        pass_on(it, s - jnp.where(has_left, SLACK + LAG * me, 0), False)
        pass_on(it, s - jnp.where(has_right, SLACK + LAG * (n - 1 - me), 0), True)
        done = s - drain
        if it == ITERS - 1:
            @pl.when((done >= 0) & (done % n == 0))
            def _():
                conclude(it, done + me)
        else:
            conclude(it, done)

    def steps(begin, end, *runs):
        def step(s, carry):
            for it, first in runs:
                advance(it, s + first)
            return carry
        lax.fori_loop(begin, end, step, 0)

    def settle(it):
        for goes_left, buf, sem in ((False, to_r, send_r), (True, to_l, send_l)):
            for place_in in range(n):
                hops = place_in if goes_left else n - 1 - place_in
                if hops == 0:
                    continue
                sent = items if it < ITERS - 1 else hops * (items // n)

                @pl.when(me == place_in)
                def _(goes_left=goes_left, buf=buf, sem=sem, sent=sent):
                    whole = buf.at[it, pl.ds(0, sent)]
                    pltpu.make_async_copy(whole, whole, sem.at[it]).wait()

    def send_smooth(it, side):
        @pl.when(there[side])
        def _():
            for piece in range(2):
                smooth_to(it, side, piece).start()

    def get_smooth(it, side, piece):
        @pl.when(there[side])
        def _():
            smooth_from(it, side, piece).wait_recv()

    def get_edge(side):
        @pl.when(there[side])
        def _():
            for h in range(MARGIN // STEP):
                for k in range(n):
                    edge_to(side, h, k, margin_at).wait_recv()

    taken = [0] * ITERS

    def until(*goals):
        runs = [[it, taken[it], max(goal, taken[it])] for it, goal in goals]
        for it, _, goal in runs:
            taken[it] = goal
        while any(at < goal for _, at, goal in runs):
            live = [run for run in runs if run[1] < run[2]]
            length = min(goal - at for _, at, goal in live)
            steps(0, length, *[(it, at) for it, at, _ in live])
            for run in live:
                run[1] += length

    def more(it, count):
        until((it, taken[it] + count))

    def factors(it, f):
        if f == 0:
            get_smooth(it, NEAR, 0)
            get_smooth(it, NEAR, 1)
        deep_last(it, f)

    def far_factors(it, part):
        get_smooth(it, FAR, part)
        deep_last(it, 3, part)

    last = planes // STEP - 2
    half = per_unit // 2
    lax.fori_loop(0, last, turn_own, 0, unroll=3)
    img_copy.wait()
    turn_halo(NEAR)
    forward(0, unit(0))
    send_smooth(0, NEAR)
    forward(0, unit(1))
    factors(0, 0)
    until((0, ahead))
    lax.fori_loop(last, planes // STEP, turn_own, 0, unroll=2)
    deep_first(0, unit(2))
    planar(0, unit(2))
    more(0, 1)
    factors(0, 1)
    more(0, 1)
    turn_halo(FAR)
    deep_first(0, unit(3))
    more(0, 1)
    planar(0, unit(3))
    send_smooth(0, FAR)
    more(0, 3)
    factors(0, 2)
    until((0, 3 * per_unit))
    far_factors(0, 0)
    until((0, 3 * per_unit + 2))

    until((0, 2 * per_unit + drain))
    get_edge(NEAR)
    deep_first(1, unit(0))
    until((0, 3 * per_unit + half))
    far_factors(0, 1)
    more(0, 1)
    planar(1, unit(0))
    send_smooth(1, NEAR)
    until((0, 3 * per_unit + drain))
    deep_first(1, unit(1))
    more(0, 1)
    planar(1, unit(1))
    more(0, 1)
    factors(1, 0)
    until((1, half), (0, taken[0] + 1))
    until((1, per_unit - 2), (0, items + drain))
    deep_first(1, unit(2))
    more(1, 1)
    planar(1, unit(2))
    more(1, 1)
    factors(1, 1)
    more(1, 2)
    get_edge(FAR)
    deep_first(1, unit(3))
    more(1, 1)
    planar(1, unit(3))
    send_smooth(1, FAR)
    more(1, 2)
    factors(1, 2)
    until((1, 3 * per_unit))
    far_factors(1, 0)
    until((1, 3 * per_unit + half))
    far_factors(1, 1)
    until((1, items + drain))
    settle(0)
    settle(1)

    for side in (NEAR, FAR):
        @pl.when(there[side])
        def _(side=side):
            est_to(side).wait_send()
            for it in range(ITERS):
                for piece in range(2):
                    smooth_to(it, side, piece).wait_send()
            for h in range(MARGIN // STEP):
                for k in range(n):
                    edge_to(side, h, k).wait_send()


def solution(mesh):
    n = mesh.shape["view"]

    def on_device(estimate, images, kernel_halves):
        planes, wx, wy = estimate.shape
        views, _, taps = kernel_halves.shape
        rows, tile = wx // n, wx * STEP
        items = n * (planes // STEP)
        deep = planes + 2 * MARGIN
        vmem = pltpu.VMEM
        dma = pltpu.SemaphoreType.DMA
        slab = vmem((wx, planes, wy), F32)
        landing = vmem((ITERS, items, rows, STEP, wy), F32)
        result = pl.pallas_call(
            functools.partial(kernel, (n, planes, wx, wy, views, taps)),
            out_shape=jax.ShapeDtypeStruct((planes * rows, wy), F32),
            in_specs=[pl.BlockSpec(memory_space=pl.ANY), pl.BlockSpec(memory_space=pl.ANY),
                      pl.BlockSpec(memory_space=pltpu.SMEM)],
            out_specs=pl.BlockSpec(memory_space=pltpu.VMEM),
            scratch_shapes=[
                vmem((ITERS, wx, deep, wy), F32),
                vmem((views, wx, UNIT, wy), F32),
                vmem((ITERS, views, wx, deep, wy), F32),
                slab, landing, landing, landing, landing,
                vmem((2, MARGIN * wx, wy), F32),
                vmem((planes * wx, wy), F32),
                vmem((views, planes * wx, wy), BF16),
                vmem((views, 3 * wy, wy), BF16),
                vmem((views, tile, 3 * tile), BF16),
                vmem((views * 4 * UNIT, 4 * (UNIT + 2 * MARGIN)), BF16),
                vmem((views * 4 * STEP, 4 * (STEP + 2 * MARGIN)), BF16),
                vmem((tile, 3 * tile), BF16),
                vmem((rows * STEP, 3 * rows * STEP), BF16),
                dma((2,)), dma((2,)), dma((2,)),
                dma((ITERS, 2, 2)), dma((ITERS, 2, 2)),
                dma((2, n * (MARGIN // STEP))), dma((2, n * (MARGIN // STEP))),
                dma((ITERS,)), dma((ITERS, items)), dma((ITERS,)), dma((ITERS, items)),
            ],
            compiler_params=pltpu.CompilerParams(
                collective_id=1, has_side_effects=True, vmem_limit_bytes=56 << 20),
            cost_estimate=pl.CostEstimate(flops=20 << 30, bytes_accessed=5 << 20, transcendentals=0),
        )(estimate.reshape(planes * wx, wy), images.reshape(views, planes * wx, wy), kernel_halves.transpose(1, 0, 2))
        return result.reshape(planes, rows, wy)

    placed = (P("space", None, None), P("view", "space", None, None), P("view", None, None))
    return jax.shard_map(
        on_device, mesh=mesh, in_specs=placed, out_specs=P("space", "view", None), check_vma=False
    )
```

```python
import functools

import jax
import jax.numpy as jnp
from jax import lax
from jax.experimental import pallas as pl
from jax.experimental.pallas import tpu as pltpu
from jax.sharding import PartitionSpec as P

ITERS = 2
MARGIN = 16
UNIT = 16
STEP = 8
LAG, SLACK = 3, 0
MESH = pl.DeviceIdType.MESH
F32, BF16 = jnp.float32, jnp.bfloat16
NEAR, FAR = 0, 1


def halved(t):
    hi = t.astype(BF16)
    return hi, (t - hi.astype(F32)).astype(BF16)


def thirds(t):
    hi = t.astype(BF16)
    rest = t - hi.astype(F32)
    mid = rest.astype(BF16)
    return hi, mid, (rest - mid.astype(F32)).astype(BF16)


def dot(a, b):
    return jnp.dot(a, b, preferred_element_type=F32)


def aligned(start, multiple=STEP):
    return start if isinstance(start, int) else pl.multiple_of(start, multiple)


def kernel(dims, est_hbm, img_hbm, halves, out, cur, mid, smooth, fac, from_l, from_r, to_r, to_l, eland, est, img,
           ty, cx, dm, dm8, pm, back, local_sem, est_send, est_recv, halo_send, halo_recv, edge_send, edge_recv,
           send_r, recv_l, send_l, recv_r):
    n, planes, wx, wy, views, taps = dims
    me = lax.axis_index("view")
    spot, spots = lax.axis_index("space"), lax.axis_size("space")
    odd = spot % 2 == 1
    toward = jnp.where(odd, -1, 1)
    there = (spot + toward < spots, (spot - toward >= 0) & (spot - toward < spots))
    who = ({"space": jnp.minimum(spot + toward, spots - 1)}, {"space": jnp.clip(spot - toward, 0, spots - 1)})
    has_left, has_right = me > 0, me < n - 1
    right = {"view": jnp.minimum(me + 1, n - 1)}
    left = {"view": jnp.maximum(me - 1, 0)}
    rows = wx // n
    tile = wx * STEP
    deep = planes + 2 * MARGIN

    def unit(f):
        return jnp.where(odd, f, planes // UNIT - 1 - f)

    margin_at = (jnp.where(odd, 0, deep - MARGIN), jnp.where(odd, deep - MARGIN, 0))
    border_at = (jnp.where(odd, MARGIN, deep - 2 * MARGIN), jnp.where(odd, deep - 2 * MARGIN, MARGIN))
    lands_at = (margin_at[FAR], margin_at[NEAR])

    est_copy = pltpu.make_async_copy(est_hbm, est, local_sem.at[0])
    img_copy = pltpu.make_async_copy(img_hbm, img, local_sem.at[1])
    est_copy.start()
    img_copy.start()

    barrier = pltpu.get_barrier_semaphore()
    count = 0
    for here, device in ((there[NEAR], who[NEAR]), (there[FAR], who[FAR]), (has_left, left), (has_right, right)):
        @pl.when(here)
        def _(device=device):
            pl.semaphore_signal(barrier, inc=1, device_id=device, device_id_type=MESH)
        count = count + here.astype(jnp.int32)

    def est_to(side):
        first = (border_at[side] - MARGIN) * wx
        return pltpu.make_async_remote_copy(
            est_hbm.at[pl.ds(aligned(first, MARGIN * wx), MARGIN * wx)], eland.at[side],
            est_send.at[side], est_recv.at[side], device_id=who[side], device_id_type=MESH)

    def piece_at(side, piece):
        return jnp.where(odd == ((side == FAR) == (piece == 0)), STEP, 0)

    def smooth_to(it, side, piece):
        off = piece_at(side, piece)
        return pltpu.make_async_remote_copy(
            smooth.at[it, :, :, pl.ds(aligned(border_at[side] + off), STEP)],
            smooth.at[it, :, :, pl.ds(aligned(lands_at[side] + off), STEP)],
            halo_send.at[it, side, piece], halo_recv.at[it, side, piece], device_id=who[side], device_id_type=MESH)

    def smooth_from(it, side, piece):
        into = smooth.at[it, :, :, pl.ds(aligned(margin_at[side] + STEP - piece_at(side, piece)), STEP)]
        return pltpu.make_async_remote_copy(
            into, into, halo_send.at[it, side, piece], halo_recv.at[it, side, piece],
            device_id=who[side], device_id_type=MESH)

    def edge_to(side, h, k, to=lands_at):
        xs = pl.ds(k * rows, rows)
        return pltpu.make_async_remote_copy(
            cur.at[1, xs, pl.ds(aligned(border_at[side] + h * STEP), STEP)],
            cur.at[1, xs, pl.ds(aligned(to[side] + h * STEP), STEP)],
            edge_send.at[side, h * n + k], edge_recv.at[side, h * n + k],
            device_id=who[side], device_id_type=MESH)

    def taps_at(distance, v, a, spacing=1):
        side = halves[a, v, 1]
        for j in range(2, taps):
            side = side + halves[a, v, j]
        total = jnp.full(distance.shape, halves[a, v, 0] + 2.0 * side)
        matrix = jnp.zeros(distance.shape, F32)
        for j in range(taps):
            matrix = jnp.where(distance == j * spacing, halves[a, v, j], matrix)
        return matrix / total

    block = 32

    def build(b, carry):
        start = pl.multiple_of(b * block, block)
        spots_in = pl.ds(start, block)
        r = lax.broadcasted_iota(jnp.int32, (block, wy), 0) + start
        c = lax.broadcasted_iota(jnp.int32, (block, wy), 1)
        for v in range(views):
            hi, lo = halved(taps_at(jnp.abs(r - c), v, 2))
            for part, value in enumerate((hi, hi, lo)):
                ty[v, pl.ds(pl.multiple_of(part * wy + start, block), block), :] = value
        r = lax.broadcasted_iota(jnp.int32, (block, tile), 0) + start
        c = lax.broadcasted_iota(jnp.int32, (block, tile), 1)
        for v in range(views):
            hi, lo = halved(taps_at(jnp.abs(r - c), v, 1, STEP))
            for part, value in enumerate((hi, hi, lo)):
                cx[v, spots_in, pl.ds(part * tile, tile)] = value
        one = jnp.where(c == (r % STEP) * wx + r // STEP, 1.0, 0.0).astype(BF16)
        for part in range(3):
            pm[spots_in, pl.ds(part * tile, tile)] = one
        return carry

    assert wy == tile
    lax.fori_loop(0, wy // block, build, 0)

    for size, into in ((UNIT, dm), (STEP, dm8)):
        width = size + 2 * MARGIN
        p = lax.broadcasted_iota(jnp.int32, (size, 4 * width), 0)
        c = lax.broadcasted_iota(jnp.int32, (size, 4 * width), 1)
        for v in range(views):
            value = taps_at(jnp.abs(c % width - MARGIN - p), v, 0)
            parts = [halved(jnp.where((c // width) % 2 == x, value, 0.0)) for x in range(2)]
            into[pl.ds(v * 4 * size, 4 * size), :] = jnp.concatenate(
                [parts[0][0], parts[1][0], parts[0][1], parts[1][1]], 0)
    window = UNIT + 2 * MARGIN
    square = rows * STEP
    r = lax.broadcasted_iota(jnp.int32, (square, 3 * square), 0)
    c = lax.broadcasted_iota(jnp.int32, (square, 3 * square), 1) % square
    back[...] = jnp.where(c == (r % rows) * STEP + r // rows, 1.0, 0.0).astype(BF16)

    pl.semaphore_wait(barrier, count)
    for side in (FAR, NEAR):
        @pl.when(there[side])
        def _(side=side):
            est_to(side).start()

    for side in (NEAR, FAR):
        @pl.when(jnp.logical_not(there[side]))
        def _(start=aligned(margin_at[side], MARGIN)):
            def clear(x, carry):
                zero = jnp.zeros((MARGIN, wy), F32)
                for it in range(ITERS):
                    cur[it, x, pl.ds(start, MARGIN), :] = zero
                    for v in range(views):
                        smooth[it, v, x, pl.ds(start, MARGIN), :] = zero
                return carry
            lax.fori_loop(0, wx, clear, 0)

    def turned(values):
        return dot(pm[...], jnp.concatenate(thirds(values), 0)).reshape(wx, STEP, wy)

    est_copy.wait()

    def turn_own(g, carry):
        b = jnp.where(odd, g, planes // STEP - 1 - g)
        values = est[pl.ds(pl.multiple_of(b * tile, tile), tile), :]
        cur[0, :, pl.ds(pl.multiple_of(MARGIN + b * STEP, STEP), STEP), :] = turned(values)
        return carry

    def turn_halo(side):
        @pl.when(there[side])
        def _():
            est_to(side).wait_recv()
            for b in range(MARGIN // STEP):
                start = aligned(margin_at[side] + b * STEP)
                cur[0, :, pl.ds(start, STEP), :] = turned(eland[side, pl.ds(b * tile, tile), :])

    def deep_first(it, u):
        def body(j, carry):
            x = 2 * j
            values = cur[it, pl.ds(x, 2), pl.ds(aligned(UNIT * u), window), :].reshape(2 * window, wy)
            got = dot(dm[...], jnp.concatenate(halved(values), 0)).reshape(views, 2, 2, UNIT, wy)
            for v in range(views):
                mid[v, pl.ds(x, 2)] = got[v, 0] + got[v, 1]
            return carry
        lax.fori_loop(0, wx // 2, body, 0, unroll=16)

    def along_y(t, v):
        hi, lo = halved(t)
        return dot(jnp.concatenate([hi, lo, hi], 1), ty[v])

    def along_x(t, v):
        hi, lo = halved(t)
        return dot(cx[v], jnp.concatenate([hi, lo, hi], 0))

    def planar(it, u):
        todo = [(v, h) for h in range(UNIT // STEP) for v in range(views)]
        ts = [mid[v, :, pl.ds(h * STEP, STEP), :].reshape(tile, wy) for v, h in todo]
        ts = [along_y(t, v) for t, (v, h) in zip(ts, todo)]
        ts = [along_x(t, v) for t, (v, h) in zip(ts, todo)]
        pics = [dot(pm[:, :tile], img[v, pl.ds(aligned((u * UNIT + h * STEP) * wx, tile), tile), :]) for v, h in todo]
        ts = [pic / t for t, pic in zip(ts, pics)]
        ts = [along_x(t, v) for t, (v, h) in zip(ts, todo)]
        ts = [along_y(t, v) for t, (v, h) in zip(ts, todo)]
        for t, (v, h) in zip(ts, todo):
            smooth[it, v, :, pl.ds(aligned(MARGIN + u * UNIT + h * STEP), STEP), :] = t.reshape(wx, STEP, wy)

    def forward(it, u):
        deep_first(it, u)
        planar(it, u)

    def deep_last(it, f, part=None):
        size, matrix = (UNIT, dm) if part is None else (STEP, dm8)
        start = unit(f) * UNIT
        if part is not None:
            start = start + jnp.where(odd == (part == 1), STEP, 0)
        width = size + 2 * MARGIN

        def body(j, carry):
            x = 2 * j
            got = []
            for v in range(views):
                values = smooth[it, v, pl.ds(x, 2), pl.ds(aligned(start), width), :].reshape(2 * width, wy)
                both = dot(matrix[pl.ds(v * 4 * size, 4 * size), :], jnp.concatenate(halved(values), 0))
                got.append(both[:2 * size] + both[2 * size:])
            product = got[0]
            for more in got[1:]:
                product = product * more
            fac[pl.ds(x, 2), pl.ds(aligned(start), size), :] = product.reshape(2, size, wy)
            return carry
        lax.fori_loop(0, wx // 2, body, 0, unroll=16)

    per_unit = n * (UNIT // STEP)
    items = n * (planes // STEP)

    def place(it, i, goes_left):
        f, h, k = i // per_unit, (i // n) % (UNIT // STEP), i % n
        if it == ITERS - 1 and not goes_left:
            k = n - 1 - k
        h = jnp.where(odd, h, UNIT // STEP - 1 - h)
        return f, h, k, pl.ds(k * rows, rows), unit(f) * UNIT + h * STEP

    def hop(it, goes_left, i):
        buf_out, buf_in, s, r, who = (
            (to_l, from_r, send_l, recv_r, left) if goes_left else (to_r, from_l, send_r, recv_l, right))
        return pltpu.make_async_remote_copy(
            buf_out.at[it, i], buf_in.at[it, i], s.at[it], r.at[it, i], device_id=who, device_id_type=MESH)

    def pass_on(it, i, goes_left):
        _, _, k, xs, first = place(it, i, goes_left)
        ps = pl.ds(aligned(first), STEP)
        live = (i >= 0) & (i < items)
        buf_out, buf_in = (to_l, from_r) if goes_left else (to_r, from_l)
        has_from, has_to = (has_right, has_left) if goes_left else (has_left, has_right)
        if it == ITERS - 1:
            wants = k <= me if goes_left else k >= me
            beyond = k < me if goes_left else k > me
        else:
            wants = beyond = True

        @pl.when(live & has_from & wants)
        def _():
            hop(it, goes_left, i).wait_recv()

        @pl.when(live & has_to & beyond)
        def _():
            @pl.when(has_from)
            def _():
                buf_out[it, i] = buf_in[it, i] * fac[xs, ps, :]

            @pl.when(jnp.logical_not(has_from))
            def _():
                buf_out[it, i] = fac[xs, ps, :]

            hop(it, goes_left, i).start()

    def conclude(it, i):
        f, h, k, xs, first = place(it, i, True)
        ps = pl.ds(aligned(first), STEP)
        inner = pl.ds(aligned(MARGIN + first), STEP)
        live = (i >= 0) & (i < items)
        from_left_at = i
        if it == ITERS - 1:
            from_left_at = i + n - 1 - 2 * k

        def finish(with_left, with_right):
            total = fac[xs, ps, :] * cur[it, xs, inner, :]
            if with_left:
                total = total * from_l[it, from_left_at]
            if with_right:
                total = total * from_r[it, i]
            if it == ITERS - 1:
                turned_back = dot(back[...], jnp.concatenate(thirds(total.reshape(rows * STEP, wy)), 0))
                out[pl.ds(aligned(first * rows), rows * STEP), :] = turned_back
            else:
                cur[it + 1, xs, inner, :] = total

        @pl.when(live & jnp.logical_not(has_left))
        def _():
            finish(False, True)

        @pl.when(live & has_left & has_right)
        def _():
            finish(True, True)

        @pl.when(live & jnp.logical_not(has_right))
        def _():
            finish(True, False)

        if it < ITERS - 1:
            for side, border in ((NEAR, 0), (FAR, planes // UNIT - 1)):
                @pl.when(live & (f == border) & there[side])
                def _(side=side):
                    edge_to(side, h, k).start()

    drain = SLACK + LAG * (n - 1)
    ahead = SLACK + LAG

    def advance(it, s):
        pass_on(it, s - jnp.where(has_left, SLACK + LAG * me, 0), False)
        pass_on(it, s - jnp.where(has_right, SLACK + LAG * (n - 1 - me), 0), True)
        done = s - drain
        if it == ITERS - 1:
            @pl.when((done >= 0) & (done % n == 0))
            def _():
                conclude(it, done + me)
        else:
            conclude(it, done)

    def steps(begin, end, *runs):
        def step(s, carry):
            for it, first in runs:
                advance(it, s + first)
            return carry
        lax.fori_loop(begin, end, step, 0)

    def settle(it):
        for goes_left, buf, sem in ((False, to_r, send_r), (True, to_l, send_l)):
            for place_in in range(n):
                hops = place_in if goes_left else n - 1 - place_in
                if hops == 0:
                    continue
                sent = items if it < ITERS - 1 else hops * (items // n)

                @pl.when(me == place_in)
                def _(goes_left=goes_left, buf=buf, sem=sem, sent=sent):
                    whole = buf.at[it, pl.ds(0, sent)]
                    pltpu.make_async_copy(whole, whole, sem.at[it]).wait()

    def send_smooth(it, side):
        @pl.when(there[side])
        def _():
            for piece in range(2):
                smooth_to(it, side, piece).start()

    def get_smooth(it, side, piece):
        @pl.when(there[side])
        def _():
            smooth_from(it, side, piece).wait_recv()

    def get_edge(side):
        @pl.when(there[side])
        def _():
            for h in range(MARGIN // STEP):
                for k in range(n):
                    edge_to(side, h, k, margin_at).wait_recv()

    taken = [0] * ITERS

    def until(*goals):
        runs = [[it, taken[it], max(goal, taken[it])] for it, goal in goals]
        for it, _, goal in runs:
            taken[it] = goal
        while any(at < goal for _, at, goal in runs):
            live = [run for run in runs if run[1] < run[2]]
            length = min(goal - at for _, at, goal in live)
            steps(0, length, *[(it, at) for it, at, _ in live])
            for run in live:
                run[1] += length

    def more(it, count):
        until((it, taken[it] + count))

    def factors(it, f):
        if f == 0:
            get_smooth(it, NEAR, 0)
            get_smooth(it, NEAR, 1)
        deep_last(it, f)

    def far_factors(it, part):
        get_smooth(it, FAR, part)
        deep_last(it, 3, part)

    last = planes // STEP - 2
    half = per_unit // 2
    lax.fori_loop(0, last, turn_own, 0, unroll=3)
    img_copy.wait()
    turn_halo(NEAR)
    forward(0, unit(0))
    send_smooth(0, NEAR)
    forward(0, unit(1))
    factors(0, 0)
    until((0, ahead + 2))
    lax.fori_loop(last, planes // STEP, turn_own, 0, unroll=2)
    deep_first(0, unit(2))
    planar(0, unit(2))
    more(0, 1)
    factors(0, 1)
    more(0, 1)
    turn_halo(FAR)
    deep_first(0, unit(3))
    more(0, 1)
    planar(0, unit(3))
    send_smooth(0, FAR)
    more(0, 3)
    factors(0, 2)
    until((0, 3 * per_unit))
    far_factors(0, 0)
    until((0, 3 * per_unit + 2))

    until((0, 2 * per_unit + drain))
    get_edge(NEAR)
    deep_first(1, unit(0))
    until((0, 3 * per_unit + half))
    far_factors(0, 1)
    more(0, 1)
    planar(1, unit(0))
    send_smooth(1, NEAR)
    until((0, 3 * per_unit + drain))
    deep_first(1, unit(1))
    more(0, 1)
    planar(1, unit(1))
    more(0, 1)
    factors(1, 0)
    until((1, half), (0, taken[0] + 1))
    until((1, per_unit - 2), (0, items + drain))
    deep_first(1, unit(2))
    more(1, 1)
    planar(1, unit(2))
    more(1, 1)
    factors(1, 1)
    more(1, 2)
    get_edge(FAR)
    deep_first(1, unit(3))
    more(1, 1)
    planar(1, unit(3))
    send_smooth(1, FAR)
    more(1, 2)
    factors(1, 2)
    until((1, 3 * per_unit))
    far_factors(1, 0)
    until((1, 3 * per_unit + half))
    far_factors(1, 1)
    until((1, items + drain))
    settle(0)
    settle(1)

    for side in (NEAR, FAR):
        @pl.when(there[side])
        def _(side=side):
            est_to(side).wait_send()
            for it in range(ITERS):
                for piece in range(2):
                    smooth_to(it, side, piece).wait_send()
            for h in range(MARGIN // STEP):
                for k in range(n):
                    edge_to(side, h, k).wait_send()


def solution(mesh):
    n = mesh.shape["view"]

    def on_device(estimate, images, kernel_halves):
        planes, wx, wy = estimate.shape
        views, _, taps = kernel_halves.shape
        rows, tile = wx // n, wx * STEP
        items = n * (planes // STEP)
        deep = planes + 2 * MARGIN
        vmem = pltpu.VMEM
        dma = pltpu.SemaphoreType.DMA
        slab = vmem((wx, planes, wy), F32)
        landing = vmem((ITERS, items, rows, STEP, wy), F32)
        result = pl.pallas_call(
            functools.partial(kernel, (n, planes, wx, wy, views, taps)),
            out_shape=jax.ShapeDtypeStruct((planes * rows, wy), F32),
            in_specs=[pl.BlockSpec(memory_space=pl.ANY), pl.BlockSpec(memory_space=pl.ANY),
                      pl.BlockSpec(memory_space=pltpu.SMEM)],
            out_specs=pl.BlockSpec(memory_space=pltpu.VMEM),
            scratch_shapes=[
                vmem((ITERS, wx, deep, wy), F32),
                vmem((views, wx, UNIT, wy), F32),
                vmem((ITERS, views, wx, deep, wy), F32),
                slab, landing, landing, landing, landing,
                vmem((2, MARGIN * wx, wy), F32),
                vmem((planes * wx, wy), F32),
                vmem((views, planes * wx, wy), BF16),
                vmem((views, 3 * wy, wy), BF16),
                vmem((views, tile, 3 * tile), BF16),
                vmem((views * 4 * UNIT, 4 * (UNIT + 2 * MARGIN)), BF16),
                vmem((views * 4 * STEP, 4 * (STEP + 2 * MARGIN)), BF16),
                vmem((tile, 3 * tile), BF16),
                vmem((rows * STEP, 3 * rows * STEP), BF16),
                dma((2,)), dma((2,)), dma((2,)),
                dma((ITERS, 2, 2)), dma((ITERS, 2, 2)),
                dma((2, n * (MARGIN // STEP))), dma((2, n * (MARGIN // STEP))),
                dma((ITERS,)), dma((ITERS, items)), dma((ITERS,)), dma((ITERS, items)),
            ],
            compiler_params=pltpu.CompilerParams(
                collective_id=1, has_side_effects=True, vmem_limit_bytes=56 << 20),
            cost_estimate=pl.CostEstimate(flops=20 << 30, bytes_accessed=5 << 20, transcendentals=0),
        )(estimate.reshape(planes * wx, wy), images.reshape(views, planes * wx, wy), kernel_halves.transpose(1, 0, 2))
        return result.reshape(planes, rows, wy)

    placed = (P("space", None, None), P("view", "space", None, None), P("view", None, None))
    return jax.shard_map(
        on_device, mesh=mesh, in_specs=placed, out_specs=P("space", "view", None), check_vma=False
    )
```
